512 devices in a mesh: dp: 16 (over x_hi, y), tile: 32 (over z, x_lo, core).
Axes of the slice: x: 4 (x_hi: 2, x_lo: 2; x = x_hi * 2 + x_lo), y: 8, z: 8, core: 2. Of those that a mesh axis runs over, the one named last changes fastest.
Arguments:
- records: bfloat16 [16, 32768, 256], P('dp', 'tile'), may hold values from -6 to 6
- obs_tile: int32 [16, 32768, 1], P('dp', 'tile'), may hold values from 0 to 31; in each aligned block of 1024 rows (0 to 1023, 1024 to 2047, ..., all dimensions but the last counted through in order) at most 128 rows name the same one
- obs_cell: int32 [16, 32768], P('dp', 'tile'), may hold values from 0 to 1023
- conv_weight: bfloat16 [2304, 384], P('dp'), may hold values from -0.125 to 0.125
- cotangent: bfloat16 [16, 128, 256, 384], P('dp', 'tile'), may hold values from -0.032958984 to 0.032958984
Outputs:
- weight_grad: float32 [2304, 384], P('dp')
The draws below stay inside these ranges and needn't reach their ends.
Inputs may be any that keep to these rules, and one draw needn't show every extreme that they name: `obs_tile`: among the 1024 records held by one device, no tile is named by more than 128 of them, a bound that some block reaches.
All inputs are finite; a program needn't handle non-finite values.
Results may differ from the reference program's by a relative error of at most 0.0035.
Values may be sent and summed in bfloat16 or wider, within the bound.
A program may use at most 64 MiB of HBM per device.

```python
import math
import jax
import jax.numpy as jnp
import numpy as np
from jax import lax

DOBS = 256
CH = 384
LON = 256
OBS_DEV = 1024
CAP = 128
BATCH = 16
TILES = 32
LAT = 128
CELLS_DEV = 1024
GRID_CELLS = 32768
OBS_TOTAL = 32768
KROWS = 2304


def with_ends(drawn, stream_key, low, high):
    longest = drawn.shape.index(max(drawn.shape))
    spots = []
    for shift in (0, 1):
        where = [jax.random.randint(jax.random.fold_in(stream_key, axis), (), 0, length) for axis, length in enumerate(drawn.shape)]
        where[longest] = (where[longest] + shift) % drawn.shape[longest]
        spots.append(tuple(where))
    return drawn.at[spots[0]].set(low).at[spots[1]].set(high)


def strengthened(result, stream_key, source, target, blocks, factor):
    owner, partner = [(jnp.arange(result.shape[position]) // (result.shape[position] // blocks)).reshape([-1 if axis == position else 1 for axis in range(result.ndim)]) for position in (source, target)]
    chosen = jax.random.permutation(stream_key, blocks)[partner]
    strong = (owner == chosen) | (owner == (partner + blocks // 2) % blocks)
    return jnp.where(strong, factor * result, result)


def shard_levels(own_key, extent, split, low, high):
    level = 1.0
    for position, blocks in split:
        draws = jax.random.uniform(jax.random.fold_in(jax.random.fold_in(own_key, 6), position), (blocks,), jnp.float32, low / len(split), high / len(split))
        level = level * jnp.repeat(jnp.exp(draws), extent[position] // blocks).reshape((-1,) + (1,) * (len(extent) - 1 - position))
    return level


def assign_block(own_key, own, number, rows, amount, top, bound, lean):
    ranking = jax.random.permutation(own_key, amount)
    heavy_load, common = shares(amount, rows * top, bound, lean, True), shares(amount, rows * top, bound, lean, False)
    places = jnp.arange(amount)

    def named(lengths, turn):
        used = int((lengths > 0).sum())
        fixed = max(1, used // 4)
        shifted = fixed + (places - fixed + turn * (used - fixed)) % max(1, amount - fixed)
        return jnp.zeros((amount,), jnp.int32).at[ranking[jnp.where(places < fixed, places, shifted)]].set(jnp.asarray(lengths, jnp.int32))

    lengths = jnp.where(number % 4 == 0, named(heavy_load, number // 4), named(common, number - number // 4 - 1))
    mixed = jax.random.permutation(jax.random.fold_in(own, 3), amount)
    donor, taker = mixed[0:amount // 2 * 2:2], mixed[1:amount // 2 * 2:2]
    room = jnp.minimum(lengths[donor] - 1, bound - lengths[taker]) // 2
    room = jnp.where((donor == ranking[0]) | (taker == ranking[0]) | (lengths[taker] == 0), 0, jnp.maximum(room, 0))
    shifted = jax.random.randint(jax.random.fold_in(own, 4), (amount // 2,), 0, 1 << 20) % (room + 1)
    lengths = lengths.at[donor].add(-shifted).at[taker].add(shifted)
    members = jnp.searchsorted(jnp.cumsum(lengths), jnp.arange(rows * top), side="right").astype(jnp.int32)
    listing = members.reshape(top, rows).T
    listing = listing[jax.random.permutation(jax.random.fold_in(own, 1), rows)]
    turn = jax.random.randint(jax.random.fold_in(own, 2), (rows, 1), 0, top)
    return jnp.take_along_axis(listing, (jnp.arange(top)[None, :] + turn) % top, axis=1)


def shares(amount, total, most, lean, full):
    weights = [(1 << 20) // math.isqrt(grade ** lean) + 1 for grade in range(1, amount + 1)]
    largest = most if full else min(most, max(-(-total // amount), total * weights[0] // sum(weights)))
    least = 1 if total - largest >= amount - 1 else 0
    given, rest = [largest] + [least] * (amount - 1), total - largest - least * (amount - 1)
    while rest > 0:
        candidates = [i for i in range(1, amount) if given[i] < largest] or [i for i in range(1, amount) if given[i] < most]
        whole, remaining = sum([weights[i] for i in candidates]), rest
        for i in candidates:
            more = min(most - given[i], max(1, remaining * weights[i] // whole), rest)
            given[i] = given[i] + more
            rest = rest - more
    return np.array(given)


def bell_draw(stream_key, extent, spread, bound, split=(), dtype=jnp.bfloat16):
    drawn = spread * jax.random.normal(stream_key, extent, jnp.float32)
    if split:
        drawn = drawn * shard_levels(stream_key, extent, split, -0.22, 0.18)
    return jnp.clip(drawn, -bound, bound).astype(dtype)


def gaussian_with(rng, dims, deviation, limit, cuts, heavy, kind=jnp.bfloat16):
    entries = deviation * jax.random.normal(rng, dims, jnp.float32)
    if cuts:
        entries = entries * shard_levels(rng, dims, cuts, -0.22, 0.18)
    return jnp.clip(strengthened(entries, jax.random.fold_in(rng, 3), *heavy), -limit, limit).astype(kind)


def setup_inputs(seed: int = 0) -> dict:
    key_of = jax.random.split(jax.random.key(seed), 6)
    records = gaussian_with(key_of[0], (BATCH, OBS_TOTAL, DOBS), 1.0, 6.0, ((0, 16), (1, 32)), (0, 2, 16, 2.0))
    obs_tile_keys = jax.random.split(jax.random.fold_in(key_of[1], 1), BATCH * OBS_TOTAL // OBS_DEV)
    obs_tile_turns = jax.random.permutation(jax.random.fold_in(key_of[1], 3), BATCH * OBS_TOTAL // OBS_DEV)
    obs_tile = jax.vmap(lambda own, number: assign_block(jax.random.fold_in(key_of[1], 2), own, number, OBS_DEV, TILES, 1, CAP, 2))(obs_tile_keys, obs_tile_turns).reshape((BATCH, OBS_TOTAL, 1))
    obs_cell = with_ends(jax.random.randint(key_of[2], (BATCH, OBS_TOTAL), 0, CELLS_DEV), jax.random.fold_in(key_of[2], 1), 0, CELLS_DEV - 1).astype(jnp.int32)
    conv_weight = bell_draw(key_of[3], (KROWS, CH), KROWS ** -0.5, 0.125, ((0, 16),))
    cotangent = bell_draw(key_of[4], (BATCH, LAT, LON, CH), (4.0 / (GRID_CELLS * BATCH) ** 0.5), 0.032958984, ((0, 16), (1, 32)))
    return dict(records=records, obs_tile=obs_tile, obs_cell=obs_cell, conv_weight=conv_weight, cotangent=cotangent)


def window_grad(records_b, tile_b, cell_b, conv_weight, cot_b):
    gcell = (tile_b[:, 0] * CELLS_DEV + cell_b).astype(jnp.int32)
    feat = jax.ops.segment_sum(records_b.astype(jnp.float32), gcell, num_segments=GRID_CELLS)
    dens = jax.ops.segment_sum(jnp.ones(gcell.shape, jnp.float32), gcell, num_segments=GRID_CELLS)
    grid = (feat / (dens[:, None] + 1.0)).astype(jnp.bfloat16).reshape(LAT, LON, DOBS)
    wrapped = jnp.concatenate([grid[:, -1:], grid, grid[:, :1]], axis=1)
    padded = jnp.pad(wrapped, ((1, 1), (0, 0), (0, 0)))
    patches = []
    for lat_off in range(3):
        for lon_off in range(3):
            patches.append(padded[lat_off:lat_off + LAT, lon_off:lon_off + LON].reshape(LAT * LON, DOBS))
    pre = jnp.zeros((LAT * LON, CH), jnp.float32)
    for tap in range(9):
        pre = pre + jnp.dot(patches[tap], conv_weight[tap * DOBS:(tap + 1) * DOBS], preferred_element_type=jnp.float32)
    _, back = jax.vjp(jax.nn.gelu, pre)
    gpre = back(cot_b.reshape(LAT * LON, CH).astype(jnp.float32))[0].astype(jnp.bfloat16)
    parts = [lax.dot_general(patches[tap], gpre, (((0,), (0,)), ((), ())), preferred_element_type=jnp.float32) for tap in range(9)]
    return jnp.concatenate(parts, axis=0)

def reference(records, obs_tile, obs_cell, conv_weight, cotangent):

    def step(total, items):
        rec_b, tile_b, cell_b, cot_b = items
        return (total + window_grad(rec_b, tile_b, cell_b, conv_weight, cot_b), None)
    start = jnp.zeros((KROWS, CH), jnp.float32)
    total, _ = lax.scan(step, start, (records, obs_tile, obs_cell, cotangent))
    return total
```

```python
import jax
import jax.numpy as jnp
from jax import lax
from jax.experimental import pallas as pl
from jax.experimental.pallas import tpu as pltpu
from jax.sharding import PartitionSpec as P

MESH = pl.DeviceIdType.MESH
F32 = jnp.float32
BF16 = jnp.bfloat16
NZ = 8
NY = 8
NT = 32
CAP = 128
ORDER = (4, 3, 5, 2, 6, 1, 7, 0)


def remote(src, dst, send, recv, where):
    return pltpu.make_async_remote_copy(
        src_ref=src, dst_ref=dst, send_sem=send, recv_sem=recv,
        device_id=where, device_id_type=MESH,
    )


def arrived(ref, sem, me):
    remote(ref, ref, sem, sem, me).wait_recv()


def front(rec_ref, tile_ref, cell_ref, w_ref, cot_ref, g_ref,
          sbuf, scell, rbuf, rcell, wbuf, xbuf, rmat, acc, dens, gp,
          rec_send, cell_send, w_send, f_send, h_send,
          rec_recv, cell_recv, w_recv, f_recv, h_recv):
    tile = lax.axis_index("tile")
    dp = lax.axis_index("dp")
    z = lax.div(tile, 4)
    kme = lax.rem(tile, 4)
    core = lax.rem(tile, 2)
    ndp = 2 * NY
    me = {"tile": tile}

    barrier = pltpu.get_barrier_semaphore()

    def greet_tile(i, _):
        pl.semaphore_signal(barrier, inc=1, device_id={"tile": lax.rem(tile + i, NT)}, device_id_type=MESH)
        return 0

    def greet_dp(i, _):
        pl.semaphore_signal(barrier, inc=1, device_id={"dp": lax.rem(dp + i, ndp)}, device_id_type=MESH)
        return 0

    lax.fori_loop(1, NT, greet_tile, 0)
    lax.fori_loop(1, ndp, greet_dp, 0)

    dest = tile_ref[...]
    marks = (lax.broadcasted_iota(jnp.int32, (NT, 1024), 0) == dest).astype(F32)
    upper = (lax.broadcasted_iota(jnp.int32, (256, 256), 0)
             < lax.broadcasted_iota(jnp.int32, (256, 256), 1)).astype(F32).astype(BF16)
    carry = jnp.zeros((NT, 1), F32)
    parts = []
    for c in range(4):
        m = marks[:, 256 * c:256 * c + 256]
        parts.append(jnp.dot(m.astype(BF16), upper, preferred_element_type=F32) + carry)
        carry = carry + jnp.sum(m, axis=1, keepdims=True)
    before = jnp.concatenate(parts, axis=1)
    pos = jnp.sum(before * marks, axis=0, keepdims=True).astype(jnp.int32)
    slot = dest * CAP + pos
    spot = (lax.broadcasted_iota(jnp.int32, (CAP, 1024), 0) == pos).astype(F32).astype(BF16)
    code = cell_ref[...] + 1
    high = jnp.right_shift(code, 5)
    low = code - high * 32
    nt = (((1,), (1,)), ((), ()))
    chigh = lax.dot_general((marks * high.astype(F32)).astype(BF16), spot, nt, preferred_element_type=F32)
    clow = lax.dot_general((marks * low.astype(F32)).astype(BF16), spot, nt, preferred_element_type=F32)
    cells = (chigh * 32.0 + clow).astype(jnp.int32) - 1
    for t in range(NT):
        scell[t] = cells[t:t + 1, :]

    def own_rows(d):
        return pl.ds(pl.multiple_of(144 * d, 16), 144)

    active = lax.rem(dp + core, 2) == 0

    @pl.when(active)
    def _():
        wbuf[own_rows(dp), :] = w_ref[...]

    pl.semaphore_wait(barrier, NT - 1 + ndp - 1)

    def w_copy(i):
        d = lax.rem(dp + i, ndp)
        return remote(w_ref, wbuf.at[own_rows(dp)], w_send.at[i], w_recv, {"dp": d})

    @pl.when(active)
    def _():
        for i in range(1, ndp):
            w_copy(i).start()

    def cell_copy(gd, k):
        t = lax.rem(z + gd, NZ) * 4 + k
        return remote(scell.at[t], rcell.at[((NZ - gd) % NZ) * 4 + kme],
                      cell_send.at[gd * 4 + k], cell_recv, {"tile": t})

    def rec_copy(gd, k):
        t = lax.rem(z + gd, NZ) * 4 + k
        g = (NZ - gd) % NZ
        return remote(sbuf.at[gd, k], rbuf.at[g, kme],
                      rec_send.at[gd * 4 + k], rec_recv.at[g], {"tile": t})

    def each(gd, act):
        for k in range(4):
            if gd == 0:
                @pl.when(k != kme)
                def _():
                    act(gd, k)
            else:
                act(gd, k)

    for gd in ORDER:
        each(gd, lambda gd, k: cell_copy(gd, k).start())

    for gd in ORDER:
        base = lax.rem(z + gd, NZ) * (4 * CAP)
        pick = (lax.broadcasted_iota(jnp.int32, (4 * CAP, 1024), 0) == (slot - base)).astype(F32).astype(BF16)
        packed = jnp.dot(pick, rec_ref[...], preferred_element_type=F32).astype(BF16)
        for k in range(4):
            sbuf[gd, k] = packed[CAP * k:CAP * k + CAP]
        each(gd, lambda gd, k: rec_copy(gd, k).start())
    rbuf[0, kme] = sbuf[0, kme]
    rcell[kme] = scell[tile]

    @pl.when(active)
    def _():
        arrived(wbuf.at[pl.ds(0, 144 * (ndp // 2 - 1))], w_recv, me)

    @pl.when(jnp.logical_not(active))
    def _():
        arrived(wbuf.at[pl.ds(0, 144 * (ndp // 2))], w_recv, me)

    partner = {"tile": tile + 1 - 2 * core}

    def f_copy(i):
        rows = own_rows(2 * i + core)
        return remote(wbuf.at[rows], wbuf.at[rows], f_send.at[i], f_recv, partner)

    for i in range(ndp // 2):
        f_copy(i).start()

    arrived(rcell.at[pl.ds(0, NT - 1)], cell_recv, me)
    acc[...] = jnp.zeros_like(acc)
    dens[...] = jnp.zeros_like(dens)
    ones = jnp.ones((4 * CAP, 128), BF16)
    for gd in ORDER:
        g = (NZ - gd) % NZ
        if g == 0:
            arrived(rbuf.at[0, pl.ds(0, 3)], rec_recv.at[0], me)
        else:
            arrived(rbuf.at[g], rec_recv.at[g], me)
        ids = jnp.concatenate([rcell[4 * g + k] for k in range(4)], axis=1)

        def chunk(r, _, g=g, ids=ids):
            start = pl.multiple_of(r * 256, 256)
            hit = (lax.broadcasted_iota(jnp.int32, (256, 4 * CAP), 0) + start == ids).astype(F32).astype(BF16)
            rows = pl.ds(start, 256)
            acc[rows, :] += jnp.dot(hit, rbuf[g].reshape(4 * CAP, 256), preferred_element_type=F32)
            dens[rows, :] += jnp.dot(hit, ones, preferred_element_type=F32)
            return 0

        lax.fori_loop(0, 4, chunk, 0)

    def spread(e, value):
        rmat[pl.ds(e * 256, 256), 0:256] = pltpu.roll(value, 1, 0).astype(BF16)
        rmat[pl.ds(e * 256, 256), 256:512] = value.astype(BF16)
        rmat[pl.ds(e * 256, 256), 512:768] = pltpu.roll(value, 255, 0).astype(BF16)

    def up_copy():
        return remote(xbuf.at[1], xbuf.at[5], h_send.at[0], h_recv.at[1], {"tile": tile - 1})

    def down_copy():
        return remote(xbuf.at[4], xbuf.at[0], h_send.at[1], h_recv.at[0], {"tile": tile + 1})

    first, last = tile == 0, tile == NT - 1

    def finish(r):
        inv = 1.0 / (dens[256 * r:256 * r + 256, :] + 1.0)
        value = acc[256 * r:256 * r + 256, :] * jnp.concatenate([inv, inv], axis=1)
        xbuf[r + 1] = value.astype(BF16)

    finish(0)

    @pl.when(jnp.logical_not(first))
    def _():
        up_copy().start()

    finish(3)

    @pl.when(jnp.logical_not(last))
    def _():
        down_copy().start()

    finish(1)
    finish(2)
    for e in range(1, 5):
        spread(e, xbuf[e].astype(F32))
    arrived(wbuf.at[pl.ds(0, 144 * (ndp // 2))], f_recv, me)

    def conv(r, n):
        pre = jnp.zeros((256 * n, 384), F32)
        for p in range(3):
            pre = pre + jnp.dot(rmat[256 * (r + p):256 * (r + p + n), :], wbuf[768 * p:768 * p + 768, :],
                                preferred_element_type=F32)
        c0 = 0.7978845608028654
        sq = pre * pre
        th = jnp.tanh(c0 * pre * (1.0 + 0.044715 * sq))
        slope = 0.5 * (1.0 + th) + 0.5 * pre * (1.0 - th * th) * (c0 * (1.0 + 3.0 * 0.044715 * sq))
        gp[256 * r:256 * (r + n), :] = (cot_ref[256 * r:256 * (r + n), :].astype(F32) * slope).astype(BF16)

    conv(1, 2)

    @pl.when(first)
    def _():
        xbuf[0] = jnp.zeros((256, 256), BF16)

    @pl.when(last)
    def _():
        xbuf[5] = jnp.zeros((256, 256), BF16)

    @pl.when(jnp.logical_not(first))
    def _():
        arrived(xbuf.at[0], h_recv.at[0], me)

    @pl.when(jnp.logical_not(last))
    def _():
        arrived(xbuf.at[5], h_recv.at[1], me)

    spread(0, xbuf[0].astype(F32))
    spread(5, xbuf[5].astype(F32))
    conv(0, 1)
    conv(3, 1)
    tn = (((0,), (0,)), ((), ()))
    for p in range(3):
        for q in range(3):
            g_ref[256 * (3 * p + q):256 * (3 * p + q) + 256, :] = lax.dot_general(
                rmat[256 * p:256 * p + 1024, 256 * q:256 * q + 256], gp[...], tn, preferred_element_type=F32)

    for gd in ORDER:
        each(gd, lambda gd, k: (cell_copy(gd, k).wait_send(), rec_copy(gd, k).wait_send()))

    @pl.when(active)
    def _():
        for i in range(1, ndp):
            w_copy(i).wait_send()

    for i in range(ndp // 2):
        f_copy(i).wait_send()

    @pl.when(jnp.logical_not(first))
    def _():
        up_copy().wait_send()

    @pl.when(jnp.logical_not(last))
    def _():
        down_copy().wait_send()


def reduce(g_ref, out_ref, s1, r1, s2, ra2, rb2, pa3, pb3, ra3, rb3, qa, qb, qf, ra4, rb4, f5,
           sends, recvs):
    tile = lax.axis_index("tile")
    dp = lax.axis_index("dp")
    z = lax.div(tile, 4)
    xlo = lax.rem(lax.div(tile, 2), 2)
    c = lax.rem(tile, 2)
    y = lax.rem(dp, NY)
    xhi = lax.div(dp, NY)
    x = xhi * 2 + xlo
    me = {"tile": tile}

    def at(xx, yy, zz, cc):
        return {"dp": lax.div(xx, 2) * NY + yy, "tile": zz * 4 + lax.rem(xx, 2) * 2 + cc}

    nsend = [0]
    started = []

    def send(cond, src, dst, recv, where):
        n = nsend[0]
        nsend[0] += 1

        def copy():
            return remote(src, dst, sends.at[n], recv, where)

        started.append((cond, copy))
        if cond is None:
            copy().start()
        else:
            @pl.when(cond)
            def _():
                copy().start()

    barrier = pltpu.get_barrier_semaphore()

    def greet(where):
        pl.semaphore_signal(barrier, inc=1, device_id=where, device_id_type=MESH)

    greet(at(x, y, z, 1 - c))
    for i in range(1, NY):
        greet(at(x, lax.rem(y + i, NY), z, c))
        greet(at(x, y, lax.rem(z + i, NZ), c))
    for i in range(1, 4):
        greet(at(lax.rem(x + i, 4), y, z, c))
    cross = lax.rem(y + c, 2) == 0
    for i in range(NY):
        yy = (y + i) % NY

        @pl.when(jnp.logical_not((yy == y) & (y == z)))
        def _(yy=yy):
            greet(at(x, yy, y, c))

    def shard(m, cc):
        h, jj = m // 4, m % 4
        return pl.ds(pl.multiple_of(144 * (NY * h + 2 * jj + cc), 16), 144)

    for m in range(8):
        s1[m] = g_ref[shard(m, 1 - c), :].astype(BF16)
    pl.semaphore_wait(barrier, 1 + 2 * (NY - 1) + 3 + NY - (y == z).astype(jnp.int32))
    for m in range(8):
        send(None, s1.at[m], r1.at[m], recvs.at[0, m], at(x, y, z, 1 - c))
    mine_a = lax.rem(y + c, 2) == 0
    mine_b = lax.rem(z + c, 2) == 0
    for jj in range(4):
        for h in range(2):
            m = 4 * h + jj
            arrived(r1.at[m], recvs.at[0, m], me)
            s2[m] = (g_ref[shard(m, c), :] + r1[m].astype(F32)).astype(BF16)
            j = 2 * jj + c
            if h == 0:
                send(j != y, s2.at[m], ra2.at[y], recvs.at[1, 0], at(x, j, z, c))

                @pl.when(j == y)
                def _(m=m):
                    ra2[y] = s2[m]
            else:
                send(j != z, s2.at[m], rb2.at[z], recvs.at[1, 1], at(x, y, j, c))

                @pl.when(j == z)
                def _(m=m):
                    rb2[z] = s2[m]

    def pieces(src, dst):
        total = src[0].astype(F32)
        for i in range(1, 8):
            total = total + src[i].astype(F32)
        stack = jnp.concatenate([total[:, 128 * b:128 * b + 128] for b in range(3)], axis=0)
        for k in range(8):
            dst[k, 0:54] = stack[54 * k:54 * k + 54]
            dst[k, 54:56] = jnp.zeros((2, 128), F32)

    @pl.when(mine_a)
    def _():
        arrived(ra2.at[pl.ds(0, 7)], recvs.at[1, 0], me)
        pieces(ra2, pa3)
        ra3[z] = pa3[z]

    for i in range(1, 8):
        zz = lax.rem(z + i, NZ)
        send(mine_a, pa3.at[zz], ra3.at[z], recvs.at[2, 0], at(x, y, zz, c))

    @pl.when(mine_b)
    def _():
        arrived(rb2.at[pl.ds(0, 7)], recvs.at[1, 1], me)
        pieces(rb2, pb3)
        rb3[y] = pb3[y]

    for i in range(1, 8):
        yy = lax.rem(y + i, NY)
        send(mine_b, pb3.at[yy], rb3.at[y], recvs.at[2, 1], at(x, yy, z, c))

    def total(src, n):
        t = src[0]
        for i in range(1, n):
            t = t + src[i]
        return t

    here_a = mine_a & (xhi == 0)
    here_b = mine_b & (xhi == 1)

    @pl.when(mine_a)
    def _():
        arrived(ra3.at[pl.ds(0, 7)], recvs.at[2, 0], me)
        qa[...] = total(ra3, 8)

    for i in range(2):
        send(mine_a & (x != i), qa, ra4.at[x], recvs.at[3, 0], at(jnp.int32(i), y, z, c))

    @pl.when(mine_b)
    def _():
        arrived(rb3.at[pl.ds(0, 7)], recvs.at[2, 1], me)
        qb[...] = total(rb3, 8)

    for i in range(2, 4):
        send(mine_b & (x != i), qb, rb4.at[x], recvs.at[3, 1], at(jnp.int32(i), y, z, c))

    @pl.when(here_a)
    def _():
        ra4[x] = qa[...]
        arrived(ra4.at[pl.ds(0, 3)], recvs.at[3, 0], me)
        f5[z] = total(ra4, 4)

    for i in range(1, 8):
        zz = lax.rem(z + i, NZ)
        send(here_a, f5.at[z], f5.at[z], recvs.at[4, 0], at(x, y, zz, c))

    @pl.when(here_b)
    def _():
        rb4[x] = qb[...]
        arrived(rb4.at[pl.ds(0, 3)], recvs.at[3, 1], me)
        qf[...] = total(rb4, 4)

    for i in range(8):
        zz = lax.rem(z + i, NZ)
        away = jnp.logical_not((y == z) & (zz == z))
        send(here_b & away, qf, f5.at[y], recvs.at[4, 1], at(x, z, zz, c))

    @pl.when(here_b & (y == z))
    def _():
        f5[y] = qf[...]

    @pl.when(here_a)
    def _():
        arrived(f5.at[pl.ds(0, 7)], recvs.at[4, 0], me)

    owner_b = mine_a & (xhi == 1)

    @pl.when(owner_b & (y == z))
    def _():
        arrived(f5.at[pl.ds(0, 7)], recvs.at[4, 1], me)

    @pl.when(owner_b & (y != z))
    def _():
        arrived(f5, recvs.at[4, 1], me)

    send(mine_a, f5, f5, recvs.at[5, 0], at(x, y, z, 1 - c))

    @pl.when(jnp.logical_not(mine_a))
    def _():
        arrived(f5, recvs.at[5, 0], me)

    stack = jnp.concatenate([f5[k, 0:54] for k in range(8)], axis=0)
    for b in range(3):
        out_ref[:, 128 * b:128 * b + 128] = stack[144 * b:144 * b + 144]

    for cond, copy in started:
        if cond is None:
            copy().wait_send()
        else:
            @pl.when(cond)
            def _(copy=copy):
                copy().wait_send()


def local(records, obs_tile, obs_cell, conv_weight, cotangent):
    vm = pl.BlockSpec(memory_space=pltpu.VMEM)
    dma = pltpu.SemaphoreType.DMA
    grad = pl.pallas_call(
        front,
        out_shape=jax.ShapeDtypeStruct((2304, 384), F32),
        in_specs=[vm] * 5,
        out_specs=vm,
        scratch_shapes=[
            pltpu.VMEM((NZ, 4, CAP, 256), BF16),
            pltpu.VMEM((NT, 1, CAP), jnp.int32),
            pltpu.VMEM((NZ, 4, CAP, 256), BF16),
            pltpu.VMEM((NT, 1, CAP), jnp.int32),
            pltpu.VMEM((2304, 384), BF16),
            pltpu.VMEM((6, 256, 256), BF16),
            pltpu.VMEM((1536, 768), BF16),
            pltpu.VMEM((1024, 256), F32),
            pltpu.VMEM((1024, 128), F32),
            pltpu.VMEM((1024, 384), BF16),
            dma((NT,)), dma((NT,)), dma((2 * NY,)), dma((NY,)), dma((2,)),
            dma((NZ,)), dma, dma, dma, dma((2,)),
        ],
        compiler_params=pltpu.CompilerParams(
            collective_id=0, has_side_effects=True, vmem_limit_bytes=50 * 1024 * 1024),
    )(records[0], obs_tile.reshape(1, 1024), obs_cell, conv_weight, cotangent.reshape(1024, 384))
    block = pltpu.VMEM((8, 144, 384), BF16)
    small = pltpu.VMEM((8, 56, 128), F32)
    piece = pltpu.VMEM((56, 128), F32)
    quad = pltpu.VMEM((4, 56, 128), F32)
    return pl.pallas_call(
        reduce,
        out_shape=jax.ShapeDtypeStruct((144, 384), F32),
        in_specs=[vm],
        out_specs=vm,
        scratch_shapes=[block] * 5 + [small] * 4 + [piece] * 3 + [quad] * 2 + [small, dma((64,)), dma((6, 8))],
        compiler_params=pltpu.CompilerParams(
            collective_id=1, has_side_effects=True, vmem_limit_bytes=50 * 1024 * 1024),
    )(grad)


def solution(mesh):
    placed = (
        P("dp", "tile", None),
        P("dp", "tile", None),
        P("dp", "tile"),
        P("dp", None),
        P("dp", "tile", None, None),
    )
    return jax.shard_map(
        local, mesh=mesh, in_specs=placed, out_specs=P("dp", None), check_vma=False
    )
```

```python
import jax
import jax.numpy as jnp
from jax import lax
from jax.experimental import pallas as pl
from jax.experimental.pallas import tpu as pltpu
from jax.sharding import PartitionSpec as P

MESH = pl.DeviceIdType.MESH
F32 = jnp.float32
BF16 = jnp.bfloat16
NZ = 8
NY = 8
NT = 32
CAP = 128
ORDER = (0, 1, 7, 2, 6, 3, 5, 4)


def remote(src, dst, send, recv, where):
    return pltpu.make_async_remote_copy(
        src_ref=src, dst_ref=dst, send_sem=send, recv_sem=recv,
        device_id=where, device_id_type=MESH,
    )


def fused(rec_hbm, tile_hbm, cell_hbm, w_hbm, cot_hbm, out_ref,
          rec, til, cel, wloc, cot,
          sbuf, scell, rbuf, rcell, wbuf, xbuf, rmat, acc, dens, gp, grad,
          s1, r1, s2a, s2b, ra2, rb2, pa3, pb3, ra3, rb3, q4, r4, f5,
          local_sem, sends, rec_recv, cell_recv, w_recv, f_recv, h_recv, recvs):
    tile = lax.axis_index("tile")
    dp = lax.axis_index("dp")
    z = lax.div(tile, 4)
    kme = lax.rem(tile, 4)
    xlo = lax.div(kme, 2)
    c = lax.rem(tile, 2)
    y = lax.rem(dp, NY)
    xhi = lax.div(dp, NY)
    x = xhi * 2 + xlo
    ndp = 2 * NY
    me = {"tile": tile}

    def at(xx, yy, zz, cc):
        return {"dp": lax.div(xx, 2) * NY + yy, "tile": zz * 4 + lax.rem(xx, 2) * 2 + cc}

    def arrived(ref, sem):
        remote(ref, ref, sem, sem, me).wait_recv()

    started = []

    def under(cond, act):
        if cond is None:
            act()
        else:
            pl.when(cond)(act)

    def send(cond, src, dst, recv, where):
        n = len(started)

        def copy():
            return remote(src, dst, sends.at[n], recv, where)

        started.append((cond, copy))
        under(cond, lambda: copy().start())

    barrier = pltpu.get_barrier_semaphore()

    def greet(where):
        pl.semaphore_signal(barrier, inc=1, device_id=where, device_id_type=MESH)

    def greet_tile(i, _):
        greet({"tile": lax.rem(tile + i, NT)})
        return 0

    def greet_dp(i, _):
        greet({"dp": lax.rem(dp + i, ndp)})
        return 0

    loads = [pltpu.make_async_copy(a, b, local_sem.at[i]) for i, (a, b) in enumerate(
        ((tile_hbm, til), (cell_hbm, cel), (rec_hbm, rec), (w_hbm, wloc), (cot_hbm, cot)))]
    for load in loads:
        load.start()
    lax.fori_loop(1, NT, greet_tile, 0)
    lax.fori_loop(1, ndp, greet_dp, 0)
    greet(at(3 - 2 * xhi - xlo, y, z, c))
    loads[0].wait()
    loads[1].wait()

    dest = til[...]
    marks = (lax.broadcasted_iota(jnp.int32, (NT, 1024), 0) == dest).astype(F32)
    upper = (lax.broadcasted_iota(jnp.int32, (256, 256), 0)
             < lax.broadcasted_iota(jnp.int32, (256, 256), 1)).astype(F32).astype(BF16)
    carry = jnp.zeros((NT, 1), F32)
    parts = []
    for i in range(4):
        m = marks[:, 256 * i:256 * i + 256]
        parts.append(jnp.dot(m.astype(BF16), upper, preferred_element_type=F32) + carry)
        carry = carry + jnp.sum(m, axis=1, keepdims=True)
    before = jnp.concatenate(parts, axis=1)
    pos = jnp.sum(before * marks, axis=0, keepdims=True).astype(jnp.int32)
    slot = dest * CAP + pos
    spot = (lax.broadcasted_iota(jnp.int32, (CAP, 1024), 0) == pos).astype(F32).astype(BF16)
    code = cel[...] + 1
    high = jnp.right_shift(code, 5)
    low = code - high * 32
    nt = (((1,), (1,)), ((), ()))
    chigh = lax.dot_general((marks * high.astype(F32)).astype(BF16), spot, nt, preferred_element_type=F32)
    clow = lax.dot_general((marks * low.astype(F32)).astype(BF16), spot, nt, preferred_element_type=F32)
    cells = (chigh * 32.0 + clow).astype(jnp.int32) - 1
    for t in range(NT):
        scell[t] = cells[t:t + 1, :]

    loads[2].wait()
    for gd in ORDER:
        base = lax.rem(z + gd, NZ) * (4 * CAP)
        pick = (lax.broadcasted_iota(jnp.int32, (4 * CAP, 1024), 0) == (slot - base)).astype(F32).astype(BF16)
        packed = jnp.dot(pick, rec[...], preferred_element_type=F32).astype(BF16)
        for k in range(4):
            sbuf[gd, k] = packed[CAP * k:CAP * k + CAP]
    loads[3].wait()

    def own_rows(d):
        return pl.ds(pl.multiple_of(144 * d, 16), 144)

    active = lax.rem(dp + c, 2) == 0
    pl.semaphore_wait(barrier, NT - 1 + ndp - 1 + 1)

    for gd in ORDER:
        t = lax.rem(z + gd, NZ) * 4
        g = (NZ - gd) % NZ
        for k in range(4):
            away = (k != kme) if gd == 0 else None
            send(away, scell.at[t + k], rcell.at[g * 4 + kme], cell_recv, {"tile": t + k})
            send(away, sbuf.at[gd, k], rbuf.at[g, kme], rec_recv.at[g], {"tile": t + k})
    for i in range(1, ndp):
        send(active, wloc, wbuf.at[own_rows(dp)], w_recv, {"dp": lax.rem(dp + i, ndp)})
    rbuf[0, kme] = sbuf[0, kme]
    rcell[kme] = scell[tile]

    @pl.when(active)
    def _():
        wbuf[own_rows(dp), :] = wloc[...]
        arrived(wbuf.at[pl.ds(0, 144 * (ndp // 2 - 1))], w_recv)

    @pl.when(jnp.logical_not(active))
    def _():
        arrived(wbuf.at[pl.ds(0, 144 * (ndp // 2))], w_recv)

    partner = at(x, y, z, 1 - c)
    for i in range(ndp // 2):
        rows = own_rows(2 * i + c)
        send(None, wbuf.at[rows], wbuf.at[rows], f_recv, partner)

    arrived(rcell.at[pl.ds(0, NT - 1)], cell_recv)
    acc[...] = jnp.zeros_like(acc)
    dens[...] = jnp.zeros_like(dens)
    ones = jnp.ones((4 * CAP, 128), BF16)

    def chunk(g, ids, start):
        hit = (lax.broadcasted_iota(jnp.int32, (256, 4 * CAP), 0) + start == ids).astype(F32).astype(BF16)
        rows = pl.ds(start, 256)
        acc[rows, :] += jnp.dot(hit, rbuf[g].reshape(4 * CAP, 256), preferred_element_type=F32)
        dens[rows, :] += jnp.dot(hit, ones, preferred_element_type=F32)

    def group(gd):
        g = (NZ - gd) % NZ
        if g == 0:
            arrived(rbuf.at[0, pl.ds(0, 3)], rec_recv.at[0])
        else:
            arrived(rbuf.at[g], rec_recv.at[g])
        return g, jnp.concatenate([rcell[4 * g + k] for k in range(4)], axis=1)

    for gd in ORDER[:-1]:
        g, ids = group(gd)

        def step(r, _, g=g, ids=ids):
            chunk(g, ids, pl.multiple_of(r * 256, 256))
            return 0

        lax.fori_loop(0, 4, step, 0)

    def spread(e):
        value = xbuf[e].astype(F32)
        rmat[pl.ds(e * 256, 256), 0:256] = pltpu.roll(value, 1, 0).astype(BF16)
        rmat[pl.ds(e * 256, 256), 256:512] = value.astype(BF16)
        rmat[pl.ds(e * 256, 256), 512:768] = pltpu.roll(value, 255, 0).astype(BF16)

    first, last = tile == 0, tile == NT - 1
    inner_top, inner_end = jnp.logical_not(first), jnp.logical_not(last)

    def finish(r):
        inv = 1.0 / (dens[256 * r:256 * r + 256, :] + 1.0)
        value = acc[256 * r:256 * r + 256, :] * jnp.concatenate([inv, inv], axis=1)
        xbuf[r + 1] = value.astype(BF16)

    g, ids = group(ORDER[-1])
    chunk(g, ids, 0)
    finish(0)
    send(inner_top, xbuf.at[1], xbuf.at[5], h_recv.at[1], {"tile": tile - 1})
    chunk(g, ids, 768)
    finish(3)
    send(inner_end, xbuf.at[4], xbuf.at[0], h_recv.at[0], {"tile": tile + 1})
    chunk(g, ids, 256)
    chunk(g, ids, 512)
    finish(1)
    finish(2)
    for e in range(1, 5):
        spread(e)
    arrived(wbuf.at[pl.ds(0, 144 * (ndp // 2))], f_recv)
    loads[4].wait()

    def conv(r, n):
        pre = jnp.zeros((256 * n, 384), F32)
        for p in range(3):
            pre = pre + jnp.dot(rmat[256 * (r + p):256 * (r + p + n), :], wbuf[768 * p:768 * p + 768, :],
                                preferred_element_type=F32)
        c0 = 0.7978845608028654
        sq = pre * pre
        th = jnp.tanh(c0 * pre * (1.0 + 0.044715 * sq))
        slope = 0.5 * (1.0 + th) + 0.5 * pre * (1.0 - th * th) * (c0 * (1.0 + 3.0 * 0.044715 * sq))
        gp[256 * r:256 * (r + n), :] = (cot[256 * r:256 * (r + n), :].astype(F32) * slope).astype(BF16)

    tn = (((0,), (0,)), ((), ()))

    def outer(r, n, p, q):
        return lax.dot_general(
            rmat[256 * (r + p):256 * (r + p + n), 256 * q:256 * q + 256], gp[256 * r:256 * (r + n), :],
            tn, preferred_element_type=F32)

    conv(1, 2)
    for p in range(3):
        for q in range(3):
            grad[256 * (3 * p + q):256 * (3 * p + q) + 256, :] = outer(1, 2, p, q)

    @pl.when(first)
    def _():
        xbuf[0] = jnp.zeros((256, 256), BF16)

    @pl.when(last)
    def _():
        xbuf[5] = jnp.zeros((256, 256), BF16)

    @pl.when(inner_top)
    def _():
        arrived(xbuf.at[0], h_recv.at[0])

    @pl.when(inner_end)
    def _():
        arrived(xbuf.at[5], h_recv.at[1])

    spread(0)
    spread(5)
    conv(0, 1)
    conv(3, 1)

    for p in range(3):
        for q in range(3):
            grad[256 * (3 * p + q):256 * (3 * p + q) + 256, :] += outer(0, 1, p, q) + outer(3, 1, p, q)
        for k in ((0, 1), (2, 3, 4), (5, 6, 7))[p]:
            s1[k] = grad[own_rows(2 * k + 1 - c), :].astype(BF16)
            send(None, s1.at[k], r1.at[k], recvs.at[k], partner)

    def stacked(value):
        return jnp.concatenate([value[:, 128 * b:128 * b + 128] for b in range(3)], axis=0)

    def paired(k):
        arrived(r1.at[k], recvs.at[k])
        return stacked(grad[own_rows(2 * k + c), :] + r1[k].astype(F32)).astype(BF16)

    for jj in range(4):
        j = 2 * jj + c
        s2a[jj, 0:432] = paired(jj)
        send(j != y, s2a.at[jj, pl.ds(0, 432)], ra2.at[y, pl.ds(0, 432)], recvs.at[8], at(x, j, z, c))

        @pl.when(j == y)
        def _(jj=jj):
            ra2[y, 0:432] = s2a[jj, 0:432]

    for jj in range(4):
        s2b[jj, 0:432] = paired(4 + jj)
        s2b[jj, 432:448] = jnp.zeros((16, 128), BF16)
    for j in range(7):
        send(j != z, s2b.at[:, pl.ds(64 * j, 64)], rb2.at[z], recvs.at[9], at(x, y, j, c))

        @pl.when(j == z)
        def _(j=j):
            rb2[j] = s2b[:, 64 * j:64 * j + 64]

    mine = lax.rem(y + c, 2) == 0
    low_z = z < 7
    both = mine & low_z

    @pl.when(mine)
    def _():
        arrived(ra2.at[pl.ds(0, 7), pl.ds(0, 432)], recvs.at[8])
        total = ra2[0, 0:432].astype(F32)
        for i in range(1, 8):
            total = total + ra2[i, 0:432].astype(F32)
        pa3[0:432] = total
        pa3[432:448] = jnp.zeros((16, 128), F32)

    for j in range(7):
        send(mine & (j != z), pa3.at[pl.ds(64 * j, 64)], ra3.at[z], recvs.at[10], at(x, y, j, c))

    @pl.when(low_z)
    def _():
        arrived(rb2.at[pl.ds(0, 7)], recvs.at[9])
        total = rb2[0].astype(F32)
        for i in range(1, 8):
            total = total + rb2[i].astype(F32)
        pb3[...] = total

    for jj in range(4):
        j = 2 * jj + c
        send(low_z & (j != y), pb3.at[jj], rb3.at[y], recvs.at[11], at(x, j, z, c))

        @pl.when(low_z & (j == y))
        def _(jj=jj):
            rb3[y] = pb3[jj]

    @pl.when(both)
    def _():
        ra3[z] = pa3[pl.ds(pl.multiple_of(64 * z, 64), 64)]
        arrived(ra3.at[pl.ds(0, 7)], recvs.at[10])
        total = ra3[0]
        for i in range(1, 8):
            total = total + ra3[i]
        q4[0] = total
        arrived(rb3.at[pl.ds(0, 7)], recvs.at[11])
        total = rb3[0]
        for i in range(1, 8):
            total = total + rb3[i]
        q4[1] = total
        r4[x] = q4[xhi]

    for i in range(1, 4):
        xx = lax.rem(x + i, 4)
        send(both, q4.at[lax.div(xx, 2)], r4.at[x], recvs.at[12], at(xx, y, z, c))

    @pl.when(both)
    def _():
        arrived(r4.at[pl.ds(0, 3)], recvs.at[12])
        f5[z] = (r4[0] + r4[1]) + (r4[2] + r4[3])

    for i in range(1, 8):
        send(both, f5.at[z], f5.at[z], recvs.at[13], at(x, y, lax.rem(z + i, NZ), c))

    @pl.when(both)
    def _():
        arrived(f5.at[pl.ds(0, 6)], recvs.at[13])

    @pl.when(mine & (z == 7))
    def _():
        arrived(f5, recvs.at[13])

    send(mine, f5, f5, recvs.at[14], partner)

    @pl.when(jnp.logical_not(mine))
    def _():
        arrived(f5, recvs.at[14])

    done = f5[...].reshape(448, 128)
    for b in range(3):
        out_ref[:, 128 * b:128 * b + 128] = done[144 * b:144 * b + 144]

    for cond, copy in started:
        under(cond, lambda copy=copy: copy().wait_send())


def local(records, obs_tile, obs_cell, conv_weight, cotangent):
    dma = pltpu.SemaphoreType.DMA
    any_space = pl.BlockSpec(memory_space=pl.ANY)

    def half(*shape):
        return pltpu.VMEM(shape, BF16)

    def full(*shape):
        return pltpu.VMEM(shape, F32)

    def ints(*shape):
        return pltpu.VMEM(shape, jnp.int32)

    return pl.pallas_call(
        fused,
        out_shape=jax.ShapeDtypeStruct((144, 384), F32),
        in_specs=[any_space] * 5,
        out_specs=pl.BlockSpec(memory_space=pltpu.VMEM),
        scratch_shapes=[
            half(1024, 256), ints(1, 1024), ints(1, 1024), half(144, 384), half(1024, 384),
            half(NZ, 4, CAP, 256), ints(NT, 1, CAP), half(NZ, 4, CAP, 256), ints(NT, 1, CAP),
            half(2304, 384), half(6, 256, 256), half(1536, 768), full(1024, 256), full(1024, 128),
            half(1024, 384), full(2304, 384),
            half(8, 144, 384), half(8, 144, 384), half(4, 448, 128), half(4, 448, 128),
            half(8, 448, 128), half(8, 4, 64, 128), full(448, 128), full(4, 64, 128),
            full(8, 64, 128), full(8, 64, 128), full(2, 64, 128), full(4, 64, 128), full(7, 64, 128),
            dma((5,)), dma((144,)), dma((NZ,)), dma, dma, dma, dma((2,)), dma((16,)),
        ],
        compiler_params=pltpu.CompilerParams(
            collective_id=0, has_side_effects=True, vmem_limit_bytes=58 * 1024 * 1024),
    )(records[0], obs_tile.reshape(1, 1024), obs_cell, conv_weight, cotangent.reshape(1024, 384))


def solution(mesh):
    placed = (
        P("dp", "tile", None),
        P("dp", "tile", None),
        P("dp", "tile"),
        P("dp", None),
        P("dp", "tile", None, None),
    )
    return jax.shard_map(
        local, mesh=mesh, in_specs=placed, out_specs=P("dp", None), check_vma=False
    )
```

```python
import jax
import jax.numpy as jnp
from jax import lax
from jax.experimental import pallas as pl
from jax.experimental.pallas import tpu as pltpu
from jax.sharding import PartitionSpec as P

MESH = pl.DeviceIdType.MESH
F32 = jnp.float32
BF16 = jnp.bfloat16
NZ = 8
NY = 8
NT = 32
CAP = 128


def remote(src, dst, send, recv, where):
    return pltpu.make_async_remote_copy(
        src_ref=src, dst_ref=dst, send_sem=send, recv_sem=recv,
        device_id=where, device_id_type=MESH,
    )


def fused(rec_hbm, tile_hbm, cell_hbm, w_hbm, cot_hbm, out_ref,
          rec, til, cel, wloc, cot,
          lout, lmeta, h1, h2, h3, h4, m1, m2, m3, m4, sbuf, scell, rbuf, rcell, wbuf, xbuf, rmat, acc, dens, gp, grad,
          s1, r1, s2a, s2b, ra2, rb2, pa3, pb3, ra3, rb3, q4, r4, f5,
          local_sem, sends, ring_recv, meta_recv, rec_recv, cell_recv, w_recv, f_recv, h_recv, recvs):
    tile = lax.axis_index("tile")
    dp = lax.axis_index("dp")
    z = lax.div(tile, 4)
    kme = lax.rem(tile, 4)
    xlo = lax.div(kme, 2)
    c = lax.rem(tile, 2)
    y = lax.rem(dp, NY)
    xhi = lax.div(dp, NY)
    x = xhi * 2 + xlo
    ndp = 2 * NY
    me = {"tile": tile}

    def at(xx, yy, zz, cc):
        return {"dp": lax.div(xx, 2) * NY + yy, "tile": zz * 4 + lax.rem(xx, 2) * 2 + cc}

    def arrived(ref, sem):
        remote(ref, ref, sem, sem, me).wait_recv()

    started = []

    def under(cond, act):
        if cond is None:
            act()
        else:
            pl.when(cond)(act)

    def send(cond, src, dst, recv, where):
        n = len(started)

        def copy():
            return remote(src, dst, sends.at[n], recv, where)

        started.append((cond, copy))
        under(cond, lambda: copy().start())

    barrier = pltpu.get_barrier_semaphore()

    def greet(where):
        pl.semaphore_signal(barrier, inc=1, device_id=where, device_id_type=MESH)

    def greet_dp(i, _):
        greet({"dp": lax.rem(dp + i, ndp)})
        return 0

    for i in (4, 3, 5, 2, 6, 1, 7):
        greet(at(x, y, lax.rem(z + i, NZ), c))
    for i in range(1, 8):
        greet(at(x, y, lax.rem(z + i, NZ), 1 - c))
    for k in range(1, 4):
        greet({"tile": z * 4 + lax.rem(kme + k, 4)})
    greet({"tile": lax.rem(tile + 1, NT)})
    greet({"tile": lax.rem(tile + NT - 1, NT)})
    lax.fori_loop(1, ndp, greet_dp, 0)
    greet(at(3 - 2 * xhi - xlo, y, z, c))
    loads = [pltpu.make_async_copy(a, b, local_sem.at[i]) for i, (a, b) in enumerate(
        ((tile_hbm, til), (cell_hbm, cel), (rec_hbm, rec), (w_hbm, wloc), (cot_hbm, cot)))]
    for load in loads:
        load.start()
    loads[0].wait()
    loads[1].wait()

    dest = til[...]
    marks = (lax.broadcasted_iota(jnp.int32, (NT, 1024), 0) == dest).astype(F32)
    upper = (lax.broadcasted_iota(jnp.int32, (256, 256), 0)
             < lax.broadcasted_iota(jnp.int32, (256, 256), 1)).astype(F32).astype(BF16)
    carry = jnp.zeros((NT, 1), F32)
    parts = []
    for i in range(4):
        m = marks[:, 256 * i:256 * i + 256]
        parts.append(jnp.dot(m.astype(BF16), upper, preferred_element_type=F32) + carry)
        carry = carry + jnp.sum(m, axis=1, keepdims=True)
    before = jnp.concatenate(parts, axis=1)
    pos = jnp.sum(before * marks, axis=0, keepdims=True).astype(jnp.int32)
    slot = dest * CAP + pos
    nt = (((1,), (1,)), ((), ()))

    def key(axis, shape, way):
        t = lax.broadcasted_iota(jnp.int32, shape, axis)
        away = jnp.bitwise_and(jnp.right_shift(t, 2) - z, 7)
        if way == 1:
            away = jnp.bitwise_and(8 - away, 7)
        limit = jnp.where(jnp.bitwise_and(t, 1) == way, 4, 3)
        return jnp.where((away >= 1) & (away <= limit), away * NT + t, -1)

    total_b = jnp.broadcast_to(carry, (NT, 128)).astype(BF16)
    spots = []
    for way in range(2):
        down, across = key(0, (NT, NT), way), key(1, (NT, NT), way)
        later = (across > down).astype(F32).astype(BF16)
        offset = jnp.dot(later, total_b, preferred_element_type=F32)[:, 0:1]
        base = jnp.where(key(0, (NT, 1), way) >= 0, 1024.0 - offset - carry, -4096.0)
        spots.append(jnp.sum((base + before) * marks, axis=0, keepdims=True).astype(jnp.int32))
    code = slot + 1
    cell = cel[...]
    traits = jnp.concatenate([
        jnp.right_shift(code, 6).astype(F32), jnp.bitwise_and(code, 63).astype(F32),
        jnp.right_shift(cell, 5).astype(F32), jnp.bitwise_and(cell, 31).astype(F32),
        jnp.zeros((4, 1024), F32)], axis=0).astype(BF16)
    loads[2].wait()

    def own_rows(d):
        return pl.ds(pl.multiple_of(144 * d, 16), 144)

    active = lax.rem(dp + c, 2) == 0
    ahead = ({"tile": lax.rem(tile + 4, NT)}, {"tile": lax.rem(tile + NT - 4, NT)})
    for i in (3, 2, 1, 0):
        for way in range(2):
            rows = pl.ds(256 * i, 256)
            perm = (lax.broadcasted_iota(jnp.int32, (256, 1024), 0) + 256 * i == spots[way]).astype(F32).astype(BF16)
            lout[way, rows] = jnp.dot(perm, rec[...], preferred_element_type=F32).astype(BF16)
            got = lax.dot_general(traits, perm, nt, preferred_element_type=F32)
            number = (got[0:1] * 64.0 + got[1:2]).astype(jnp.int32) - 1
            lmeta[way, :, rows] = number * 1024 + (got[2:3] * 32.0 + got[3:4]).astype(jnp.int32)
            if i == 3 and way == 0:
                pl.semaphore_wait(barrier, 14 + 3 + 2 + ndp - 1 + 1)
            send(None, lout.at[way, rows], h1.at[way, rows], ring_recv.at[way, i], ahead[way])
    for way in range(2):
        send(None, lmeta.at[way], m1.at[way], meta_recv.at[way, 0], ahead[way])
    loads[3].wait()
    for i in range(1, ndp):
        send(active, wloc, wbuf.at[own_rows(dp)], w_recv, {"dp": lax.rem(dp + i, ndp)})
    def share(g, data, number, cell_id):
        length = number.shape[1]
        rel = number - 512 * z
        pick = (lax.broadcasted_iota(jnp.int32, (4 * CAP, length), 0) == rel).astype(F32).astype(BF16)
        packed = jnp.dot(pick, data, preferred_element_type=F32).astype(BF16)
        owner = (lax.broadcasted_iota(jnp.int32, (8, length), 0) == jnp.right_shift(rel, 7)).astype(F32)
        spot = (lax.broadcasted_iota(jnp.int32, (CAP, length), 0) == jnp.bitwise_and(rel, 127)).astype(F32).astype(BF16)
        cell_code = cell_id + 1
        high = jnp.right_shift(cell_code, 5).astype(F32)
        low = jnp.bitwise_and(cell_code, 31).astype(F32)
        chigh = lax.dot_general((owner * high).astype(BF16), spot, nt, preferred_element_type=F32)
        clow = lax.dot_general((owner * low).astype(BF16), spot, nt, preferred_element_type=F32)
        cells = (chigh * 32.0 + clow).astype(jnp.int32) - 1
        for k in range(4):
            scell[4 * g + k] = cells[k:k + 1, :]
            sbuf[g, k] = packed[CAP * k:CAP * k + CAP]
        for k in range(4):
            there = {"tile": z * 4 + k}
            send(k != kme, sbuf.at[g, k], rbuf.at[g, kme], rec_recv.at[g], there)
            send(k != kme, scell.at[4 * g + k], rcell.at[4 * g + kme], cell_recv.at[g], there)
        rbuf[g, kme] = sbuf[g, kme]
        rcell[4 * g + kme] = scell[4 * g + kme]

    def share_list(g, data, meta):
        share(g, data, jnp.right_shift(meta, 10), jnp.bitwise_and(meta, 1023))

    acc[...] = jnp.zeros_like(acc)
    dens[...] = jnp.zeros_like(dens)
    ones = jnp.ones((4 * CAP, 128), BF16)

    def chunk(g, ids, start):
        hit = (lax.broadcasted_iota(jnp.int32, (256, 4 * CAP), 0) + start == ids).astype(F32).astype(BF16)
        rows = pl.ds(start, 256)
        acc[rows, :] += jnp.dot(hit, rbuf[g].reshape(4 * CAP, 256), preferred_element_type=F32)
        dens[rows, :] += jnp.dot(hit, ones, preferred_element_type=F32)

    def group(g):
        arrived(rcell.at[pl.ds(4 * g, 3)], cell_recv.at[g])
        arrived(rbuf.at[g, pl.ds(0, 3)], rec_recv.at[g])
        return jnp.concatenate([rcell[4 * g + k] for k in range(4)], axis=1)

    def into_cells(g):
        ids = group(g)

        def step(r, _):
            chunk(g, ids, pl.multiple_of(r * 256, 256))
            return 0

        lax.fori_loop(0, 4, step, 0)

    share(0, rec[...], slot, cell)

    for way in range(2):
        arrived(m1.at[way], meta_recv.at[way, 0])
        send(None, m1.at[way], m2.at[way], meta_recv.at[way, 1], ahead[way])
    for i in (3, 2, 1, 0):
        rows = pl.ds(256 * i, 256)
        for way in range(2):
            arrived(h1.at[way, rows], ring_recv.at[way, i])
            send(None, h1.at[way, rows], h2.at[way, rows], ring_recv.at[way, 4 + i], ahead[way])
    for way in range(2):
        share_list(1 + way, h1[way], m1[way])
    into_cells(0)

    for way in range(2):
        arrived(m2.at[way], meta_recv.at[way, 1])
        send(None, m2.at[way], m3.at[way], meta_recv.at[way, 2], ahead[way])
    for i in (3, 2, 1, 0):
        rows = pl.ds(256 * i, 256)
        for way in range(2):
            arrived(h2.at[way, rows], ring_recv.at[way, 4 + i])
            if i > 0:
                send(None, h2.at[way, rows], h3.at[way, pl.ds(256 * i - 256, 256)], ring_recv.at[way, 8 + i], ahead[way])
    for way in range(2):
        share_list(3 + way, h2[way], m2[way])
    into_cells(1)
    into_cells(2)

    @pl.when(active)
    def _():
        wbuf[own_rows(dp), :] = wloc[...]
        arrived(wbuf.at[pl.ds(0, 144 * (ndp // 2 - 1))], w_recv)

    @pl.when(jnp.logical_not(active))
    def _():
        arrived(wbuf.at[pl.ds(0, 144 * (ndp // 2))], w_recv)

    partner = at(x, y, z, 1 - c)
    for i in range(ndp // 2):
        rows = own_rows(2 * i + c)
        send(None, wbuf.at[rows], wbuf.at[rows], f_recv, partner)

    for way in range(2):
        arrived(m3.at[way], meta_recv.at[way, 2])
        send(None, m3.at[way], m4.at[way], meta_recv.at[way, 3], ahead[way])
    for i in (3, 2, 1):
        rows = pl.ds(256 * i - 256, 256)
        for way in range(2):
            arrived(h3.at[way, rows], ring_recv.at[way, 8 + i])
            if i == 3:
                send(None, h3.at[way, rows], h4.at[way], ring_recv.at[way, 8], ahead[way])
    for way in range(2):
        share_list(5 + way, h3[way], m3[way][:, 256:1024])
    into_cells(3)
    into_cells(4)
    for way in range(2):
        arrived(m4.at[way], meta_recv.at[way, 3])
        arrived(h4.at[way], ring_recv.at[way, 8])
    share_list(7, h4[...].reshape(512, 256),
               jnp.concatenate([m4[0][:, 768:1024], m4[1][:, 768:1024]], axis=1))
    into_cells(5)
    into_cells(6)

    def spread(e):
        value = xbuf[e].astype(F32)
        rmat[pl.ds(e * 256, 256), 0:256] = pltpu.roll(value, 1, 0).astype(BF16)
        rmat[pl.ds(e * 256, 256), 256:512] = value.astype(BF16)
        rmat[pl.ds(e * 256, 256), 512:768] = pltpu.roll(value, 255, 0).astype(BF16)

    first, last = tile == 0, tile == NT - 1
    inner_top, inner_end = jnp.logical_not(first), jnp.logical_not(last)

    def finish(r):
        inv = 1.0 / (dens[256 * r:256 * r + 256, :] + 1.0)
        value = acc[256 * r:256 * r + 256, :] * jnp.concatenate([inv, inv], axis=1)
        xbuf[r + 1] = value.astype(BF16)

    g = 7
    ids = group(g)
    chunk(g, ids, 0)
    finish(0)
    send(inner_top, xbuf.at[1], xbuf.at[5], h_recv.at[1], {"tile": tile - 1})
    chunk(g, ids, 768)
    finish(3)
    send(inner_end, xbuf.at[4], xbuf.at[0], h_recv.at[0], {"tile": tile + 1})
    chunk(g, ids, 256)
    chunk(g, ids, 512)
    finish(1)
    finish(2)
    for e in range(1, 5):
        spread(e)
    arrived(wbuf.at[pl.ds(0, 144 * (ndp // 2))], f_recv)
    loads[4].wait()

    def conv(r, n):
        pre = jnp.zeros((256 * n, 384), F32)
        for p in range(3):
            pre = pre + jnp.dot(rmat[256 * (r + p):256 * (r + p + n), :], wbuf[768 * p:768 * p + 768, :],
                                preferred_element_type=F32)
        c0 = 0.7978845608028654
        sq = pre * pre
        th = jnp.tanh(c0 * pre * (1.0 + 0.044715 * sq))
        slope = 0.5 * (1.0 + th) + 0.5 * pre * (1.0 - th * th) * (c0 * (1.0 + 3.0 * 0.044715 * sq))
        gp[256 * r:256 * (r + n), :] = (cot[256 * r:256 * (r + n), :].astype(F32) * slope).astype(BF16)

    tn = (((0,), (0,)), ((), ()))

    def outer(r, n, p, q):
        return lax.dot_general(
            rmat[256 * (r + p):256 * (r + p + n), 256 * q:256 * q + 256], gp[256 * r:256 * (r + n), :],
            tn, preferred_element_type=F32)

    conv(1, 2)
    for p in range(3):
        for q in range(3):
            grad[256 * (3 * p + q):256 * (3 * p + q) + 256, :] = outer(1, 2, p, q)

    @pl.when(first)
    def _():
        xbuf[0] = jnp.zeros((256, 256), BF16)

    @pl.when(last)
    def _():
        xbuf[5] = jnp.zeros((256, 256), BF16)

    @pl.when(inner_top)
    def _():
        arrived(xbuf.at[0], h_recv.at[0])

    @pl.when(inner_end)
    def _():
        arrived(xbuf.at[5], h_recv.at[1])

    spread(0)
    spread(5)
    conv(0, 1)
    conv(3, 1)

    for p in range(3):
        for q in range(3):
            grad[256 * (3 * p + q):256 * (3 * p + q) + 256, :] += outer(0, 1, p, q) + outer(3, 1, p, q)
        for k in ((0, 1), (2, 3, 4), (5, 6, 7))[p]:
            s1[k] = grad[own_rows(2 * k + 1 - c), :].astype(BF16)
            send(None, s1.at[k], r1.at[k], recvs.at[k], partner)

    def stacked(value):
        return jnp.concatenate([value[:, 128 * b:128 * b + 128] for b in range(3)], axis=0)

    def paired(k):
        arrived(r1.at[k], recvs.at[k])
        return stacked(grad[own_rows(2 * k + c), :] + r1[k].astype(F32)).astype(BF16)

    for jj in range(4):
        j = 2 * jj + c
        s2a[jj, 0:432] = paired(jj)
        send(j != y, s2a.at[jj, pl.ds(0, 432)], ra2.at[y, pl.ds(0, 432)], recvs.at[8], at(x, j, z, c))

        @pl.when(j == y)
        def _(jj=jj):
            ra2[y, 0:432] = s2a[jj, 0:432]

    for jj in range(4):
        s2b[jj, 0:432] = paired(4 + jj)
        s2b[jj, 432:448] = jnp.zeros((16, 128), BF16)
    for j in range(7):
        send(j != z, s2b.at[:, pl.ds(64 * j, 64)], rb2.at[z], recvs.at[9], at(x, y, j, c))

        @pl.when(j == z)
        def _(j=j):
            rb2[j] = s2b[:, 64 * j:64 * j + 64]

    mine = lax.rem(y + c, 2) == 0
    low_z = z < 7
    both = mine & low_z

    @pl.when(mine)
    def _():
        arrived(ra2.at[pl.ds(0, 7), pl.ds(0, 432)], recvs.at[8])
        total = ra2[0, 0:432].astype(F32)
        for i in range(1, 8):
            total = total + ra2[i, 0:432].astype(F32)
        pa3[0:432] = total
        pa3[432:448] = jnp.zeros((16, 128), F32)

    for j in range(7):
        send(mine & (j != z), pa3.at[pl.ds(64 * j, 64)], ra3.at[z], recvs.at[10], at(x, y, j, c))

    @pl.when(low_z)
    def _():
        arrived(rb2.at[pl.ds(0, 7)], recvs.at[9])
        total = rb2[0].astype(F32)
        for i in range(1, 8):
            total = total + rb2[i].astype(F32)
        pb3[...] = total

    for jj in range(4):
        j = 2 * jj + c
        send(low_z & (j != y), pb3.at[jj], rb3.at[y], recvs.at[11], at(x, j, z, c))

        @pl.when(low_z & (j == y))
        def _(jj=jj):
            rb3[y] = pb3[jj]

    @pl.when(both)
    def _():
        ra3[z] = pa3[pl.ds(pl.multiple_of(64 * z, 64), 64)]
        arrived(ra3.at[pl.ds(0, 7)], recvs.at[10])
        total = ra3[0]
        for i in range(1, 8):
            total = total + ra3[i]
        q4[0] = total
        arrived(rb3.at[pl.ds(0, 7)], recvs.at[11])
        total = rb3[0]
        for i in range(1, 8):
            total = total + rb3[i]
        q4[1] = total
        r4[x] = q4[xhi]

    for i in range(1, 4):
        xx = lax.rem(x + i, 4)
        send(both, q4.at[lax.div(xx, 2)], r4.at[x], recvs.at[12], at(xx, y, z, c))

    @pl.when(both)
    def _():
        arrived(r4.at[pl.ds(0, 3)], recvs.at[12])
        f5[z] = ((r4[0] + r4[1]) + (r4[2] + r4[3])).astype(BF16)

    for i in range(8):
        zz = lax.rem(z + i, NZ)
        for cc in ((1 - c,) if i == 0 else (c, 1 - c)):
            send(both, f5.at[z], f5.at[z], recvs.at[13], at(x, y, zz, cc))

    @pl.when(both)
    def _():
        arrived(f5.at[pl.ds(0, 6)], recvs.at[13])

    @pl.when(jnp.logical_not(both))
    def _():
        arrived(f5, recvs.at[13])

    done = f5[...].astype(F32).reshape(448, 128)
    for b in range(3):
        out_ref[:, 128 * b:128 * b + 128] = done[144 * b:144 * b + 144]

    for cond, copy in started:
        under(cond, lambda copy=copy: copy().wait_send())


def local(records, obs_tile, obs_cell, conv_weight, cotangent):
    dma = pltpu.SemaphoreType.DMA
    any_space = pl.BlockSpec(memory_space=pl.ANY)

    def half(*shape):
        return pltpu.VMEM(shape, BF16)

    def full(*shape):
        return pltpu.VMEM(shape, F32)

    def ints(*shape):
        return pltpu.VMEM(shape, jnp.int32)

    return pl.pallas_call(
        fused,
        out_shape=jax.ShapeDtypeStruct((144, 384), F32),
        in_specs=[any_space] * 5,
        out_specs=pl.BlockSpec(memory_space=pltpu.VMEM),
        scratch_shapes=[
            half(1024, 256), ints(1, 1024), ints(1, 1024), half(144, 384), half(1024, 384),
            half(2, 1024, 256), ints(2, 1, 1024), half(2, 1024, 256), half(2, 1024, 256), half(2, 768, 256),
            half(2, 256, 256), ints(2, 1, 1024), ints(2, 1, 1024), ints(2, 1, 1024), ints(2, 1, 1024),
            half(NZ, 4, CAP, 256), ints(NT, 1, CAP), half(NZ, 4, CAP, 256), ints(NT, 1, CAP),
            half(2304, 384), half(6, 256, 256), half(1536, 768), full(1024, 256), full(1024, 128),
            half(1024, 384), full(2304, 384),
            half(8, 144, 384), half(8, 144, 384), half(4, 448, 128), half(4, 448, 128),
            half(8, 448, 128), half(8, 4, 64, 128), full(448, 128), full(4, 64, 128),
            full(8, 64, 128), full(8, 64, 128), full(2, 64, 128), full(4, 64, 128), half(7, 64, 128),
            dma((5,)), dma((200,)), dma((2, 12)), dma((2, 4)), dma((NZ,)), dma((NZ,)), dma, dma, dma((2,)), dma((16,)),
        ],
        compiler_params=pltpu.CompilerParams(
            collective_id=0, has_side_effects=True, vmem_limit_bytes=58 * 1024 * 1024),
    )(records[0], obs_tile.reshape(1, 1024), obs_cell, conv_weight, cotangent.reshape(1024, 384))


def solution(mesh):
    placed = (
        P("dp", "tile", None),
        P("dp", "tile", None),
        P("dp", "tile"),
        P("dp", None),
        P("dp", "tile", None, None),
    )
    return jax.shard_map(
        local, mesh=mesh, in_specs=placed, out_specs=P("dp", None), check_vma=False
    )
```

```python
import jax
import jax.numpy as jnp
from jax import lax
from jax.experimental import pallas as pl
from jax.experimental.pallas import tpu as pltpu
from jax.sharding import PartitionSpec as P

MESH = pl.DeviceIdType.MESH
F32 = jnp.float32
BF16 = jnp.bfloat16
NZ = 8
NY = 8
NT = 32
CAP = 128


def remote(src, dst, send, recv, where):
    return pltpu.make_async_remote_copy(
        src_ref=src, dst_ref=dst, send_sem=send, recv_sem=recv,
        device_id=where, device_id_type=MESH,
    )


def fused(rec_hbm, tile_hbm, cell_hbm, w_hbm, cot_hbm, out_ref,
          rec, til, cel, wloc, cot,
          lout, lmeta, h1, h2, h3, h4, m1, m2, m3, m4, sbuf, scell, rbuf, rcell, wbuf, xbuf, rmat, acc, dens, gp, grad,
          s2, ra2, rb2, p3, r3, q4, r4, f5,
          local_sem, sends, ring_recv, meta_recv, rec_recv, cell_recv, w_recv, f_recv, h_recv, x_recv, g_recv, recvs):
    tile = lax.axis_index("tile")
    dp = lax.axis_index("dp")
    z = lax.div(tile, 4)
    kme = lax.rem(tile, 4)
    xlo = lax.div(kme, 2)
    c = lax.rem(tile, 2)
    y = lax.rem(dp, NY)
    xhi = lax.div(dp, NY)
    x = xhi * 2 + xlo
    ndp = 2 * NY
    me = {"tile": tile}

    def at(xx, yy, zz, cc):
        return {"dp": lax.div(xx, 2) * NY + yy, "tile": zz * 4 + lax.rem(xx, 2) * 2 + cc}

    def arrived(ref, sem):
        remote(ref, ref, sem, sem, me).wait_recv()

    started = []

    def under(cond, act):
        if cond is None:
            act()
        else:
            pl.when(cond)(act)

    def send(cond, src, dst, recv, where):
        n = len(started)

        def copy():
            return remote(src, dst, sends.at[n], recv, where)

        started.append((cond, copy))
        under(cond, lambda: copy().start())

    barrier = pltpu.get_barrier_semaphore()

    def greet(where):
        pl.semaphore_signal(barrier, inc=1, device_id=where, device_id_type=MESH)

    def greet_dp(i, _):
        greet({"dp": lax.rem(dp + i, ndp)})
        return 0

    for i in (4, 3, 5, 2, 6, 1, 7):
        greet(at(x, y, lax.rem(z + i, NZ), c))
    for i in range(1, 8):
        greet(at(x, y, lax.rem(z + i, NZ), 1 - c))
    for k in range(1, 4):
        greet({"tile": z * 4 + lax.rem(kme + k, 4)})
    greet({"tile": lax.rem(tile + 1, NT)})
    greet({"tile": lax.rem(tile + NT - 1, NT)})
    lax.fori_loop(1, ndp, greet_dp, 0)
    greet(at(3 - 2 * xhi - xlo, y, z, c))
    loads = [pltpu.make_async_copy(a, b, local_sem.at[i]) for i, (a, b) in enumerate(
        ((tile_hbm, til), (cell_hbm, cel), (rec_hbm, rec), (w_hbm, wloc), (cot_hbm, cot)))]
    for load in loads:
        load.start()
    loads[0].wait()
    loads[1].wait()

    dest = til[...]
    marks = (lax.broadcasted_iota(jnp.int32, (NT, 1024), 0) == dest).astype(F32)
    upper = (lax.broadcasted_iota(jnp.int32, (256, 256), 0)
             < lax.broadcasted_iota(jnp.int32, (256, 256), 1)).astype(F32).astype(BF16)
    carry = jnp.zeros((NT, 1), F32)
    parts = []
    for i in range(4):
        m = marks[:, 256 * i:256 * i + 256]
        parts.append(jnp.dot(m.astype(BF16), upper, preferred_element_type=F32) + carry)
        carry = carry + jnp.sum(m, axis=1, keepdims=True)
    before = jnp.concatenate(parts, axis=1)
    pos = jnp.sum(before * marks, axis=0, keepdims=True).astype(jnp.int32)
    slot = dest * CAP + pos
    nt = (((1,), (1,)), ((), ()))

    def key(axis, shape, way):
        t = lax.broadcasted_iota(jnp.int32, shape, axis)
        away = jnp.bitwise_and(jnp.right_shift(t, 2) - z, 7)
        if way == 1:
            away = jnp.bitwise_and(8 - away, 7)
        limit = jnp.where(jnp.bitwise_and(t, 1) == way, 4, 3)
        return jnp.where((away >= 1) & (away <= limit), away * NT + t, -1)

    total_b = jnp.broadcast_to(carry, (NT, 128)).astype(BF16)
    spots = []
    for way in range(2):
        down, across = key(0, (NT, NT), way), key(1, (NT, NT), way)
        later = (across > down).astype(F32).astype(BF16)
        offset = jnp.dot(later, total_b, preferred_element_type=F32)[:, 0:1]
        base = jnp.where(key(0, (NT, 1), way) >= 0, 1024.0 - offset - carry, -4096.0)
        spots.append(jnp.sum((base + before) * marks, axis=0, keepdims=True).astype(jnp.int32))
    code = slot + 1
    cell = cel[...]
    traits = jnp.concatenate([
        jnp.right_shift(code, 6).astype(F32), jnp.bitwise_and(code, 63).astype(F32),
        jnp.right_shift(cell, 5).astype(F32), jnp.bitwise_and(cell, 31).astype(F32),
        jnp.zeros((4, 1024), F32)], axis=0).astype(BF16)
    loads[2].wait()

    def own_rows(d):
        return pl.ds(pl.multiple_of(144 * d, 16), 144)

    active = lax.rem(dp + c, 2) == 0
    ahead = ({"tile": lax.rem(tile + 4, NT)}, {"tile": lax.rem(tile + NT - 4, NT)})
    for i in (3, 2, 1, 0):
        for way in range(2):
            rows = pl.ds(256 * i, 256)
            perm = (lax.broadcasted_iota(jnp.int32, (256, 1024), 0) + 256 * i == spots[way]).astype(F32).astype(BF16)
            lout[way, rows] = jnp.dot(perm, rec[...], preferred_element_type=F32).astype(BF16)
            got = lax.dot_general(traits, perm, nt, preferred_element_type=F32)
            number = (got[0:1] * 64.0 + got[1:2]).astype(jnp.int32) - 1
            lmeta[way, :, rows] = number * 1024 + (got[2:3] * 32.0 + got[3:4]).astype(jnp.int32)
            if i == 3 and way == 0:
                pl.semaphore_wait(barrier, 14 + 3 + 2 + ndp - 1 + 1)
            send(None, lout.at[way, rows], h1.at[way, rows], ring_recv.at[way, i], ahead[way])
    for way in range(2):
        send(None, lmeta.at[way], m1.at[way], meta_recv.at[way, 0], ahead[way])
    loads[3].wait()
    for i in range(1, ndp):
        send(active, wloc, wbuf.at[own_rows(dp)], w_recv, {"dp": lax.rem(dp + i, ndp)})
    def share(g, data, number, cell_id):
        length = number.shape[1]
        rel = number - 512 * z
        pick = (lax.broadcasted_iota(jnp.int32, (4 * CAP, length), 0) == rel).astype(F32).astype(BF16)
        packed = jnp.dot(pick, data, preferred_element_type=F32).astype(BF16)
        owner = (lax.broadcasted_iota(jnp.int32, (8, length), 0) == jnp.right_shift(rel, 7)).astype(F32)
        spot = (lax.broadcasted_iota(jnp.int32, (CAP, length), 0) == jnp.bitwise_and(rel, 127)).astype(F32).astype(BF16)
        cell_code = cell_id + 1
        high = jnp.right_shift(cell_code, 5).astype(F32)
        low = jnp.bitwise_and(cell_code, 31).astype(F32)
        chigh = lax.dot_general((owner * high).astype(BF16), spot, nt, preferred_element_type=F32)
        clow = lax.dot_general((owner * low).astype(BF16), spot, nt, preferred_element_type=F32)
        cells = (chigh * 32.0 + clow).astype(jnp.int32) - 1
        for k in range(4):
            scell[4 * g + k] = cells[k:k + 1, :]
            sbuf[g, k] = packed[CAP * k:CAP * k + CAP]
        for k in range(4):
            there = {"tile": z * 4 + k}
            send(k != kme, sbuf.at[g, k], rbuf.at[g, kme], rec_recv.at[g], there)
            send(k != kme, scell.at[4 * g + k], rcell.at[4 * g + kme], cell_recv.at[g], there)
        rbuf[g, kme] = sbuf[g, kme]
        rcell[4 * g + kme] = scell[4 * g + kme]

    def share_list(g, data, meta):
        share(g, data, jnp.right_shift(meta, 10), jnp.bitwise_and(meta, 1023))

    acc[...] = jnp.zeros_like(acc)
    dens[...] = jnp.zeros_like(dens)
    ones = jnp.ones((4 * CAP, 128), BF16)

    def chunk(g, ids, start):
        hit = (lax.broadcasted_iota(jnp.int32, (256, 4 * CAP), 0) + start == ids).astype(F32).astype(BF16)
        rows = pl.ds(start, 256)
        acc[rows, :] += jnp.dot(hit, rbuf[g].reshape(4 * CAP, 256), preferred_element_type=F32)
        dens[rows, :] += jnp.dot(hit, ones, preferred_element_type=F32)

    def group(g):
        arrived(rcell.at[pl.ds(4 * g, 3)], cell_recv.at[g])
        arrived(rbuf.at[g, pl.ds(0, 3)], rec_recv.at[g])
        return jnp.concatenate([rcell[4 * g + k] for k in range(4)], axis=1)

    def into_cells(g):
        ids = group(g)

        def step(r, _):
            chunk(g, ids, pl.multiple_of(r * 256, 256))
            return 0

        lax.fori_loop(0, 4, step, 0)

    share(0, rec[...], slot, cell)

    for way in range(2):
        arrived(m1.at[way], meta_recv.at[way, 0])
        send(None, m1.at[way], m2.at[way], meta_recv.at[way, 1], ahead[way])
    for i in (3, 2, 1, 0):
        rows = pl.ds(256 * i, 256)
        for way in range(2):
            arrived(h1.at[way, rows], ring_recv.at[way, i])
            send(None, h1.at[way, rows], h2.at[way, rows], ring_recv.at[way, 4 + i], ahead[way])
    for way in range(2):
        share_list(1 + way, h1[way], m1[way])
    into_cells(0)

    for way in range(2):
        arrived(m2.at[way], meta_recv.at[way, 1])
        send(None, m2.at[way], m3.at[way], meta_recv.at[way, 2], ahead[way])
    for i in (3, 2, 1, 0):
        rows = pl.ds(256 * i, 256)
        for way in range(2):
            arrived(h2.at[way, rows], ring_recv.at[way, 4 + i])
            if i > 0:
                send(None, h2.at[way, rows], h3.at[way, pl.ds(256 * i - 256, 256)], ring_recv.at[way, 8 + i], ahead[way])
    for way in range(2):
        share_list(3 + way, h2[way], m2[way])
    into_cells(1)
    into_cells(2)

    @pl.when(active)
    def _():
        wbuf[own_rows(dp), :] = wloc[...]
        arrived(wbuf.at[pl.ds(0, 144 * (ndp // 2 - 1))], w_recv)

    @pl.when(jnp.logical_not(active))
    def _():
        arrived(wbuf.at[pl.ds(0, 144 * (ndp // 2))], w_recv)

    partner = at(x, y, z, 1 - c)
    for i in range(ndp // 2):
        rows = own_rows(2 * i + c)
        send(None, wbuf.at[rows], wbuf.at[rows], f_recv, partner)

    for way in range(2):
        arrived(m3.at[way], meta_recv.at[way, 2])
        send(None, m3.at[way], m4.at[way], meta_recv.at[way, 3], ahead[way])
    for i in (3, 2, 1):
        rows = pl.ds(256 * i - 256, 256)
        for way in range(2):
            arrived(h3.at[way, rows], ring_recv.at[way, 8 + i])
            if i == 3:
                send(None, h3.at[way, rows], h4.at[way], ring_recv.at[way, 8], ahead[way])
    for way in range(2):
        share_list(5 + way, h3[way], m3[way][:, 256:1024])
    into_cells(3)
    into_cells(4)
    for way in range(2):
        arrived(m4.at[way], meta_recv.at[way, 3])
        arrived(h4.at[way], ring_recv.at[way, 8])
    share_list(7, h4[...].reshape(512, 256),
               jnp.concatenate([m4[0][:, 768:1024], m4[1][:, 768:1024]], axis=1))
    into_cells(5)
    into_cells(6)

    def block(n, size=256, count=1):
        return pl.ds(pl.multiple_of(n * size, size), size * count)

    def spread(e):
        value = xbuf[e].astype(F32)
        rmat[block(e), 0:256] = pltpu.roll(value, 1, 0).astype(BF16)
        rmat[block(e), 256:512] = value.astype(BF16)
        rmat[block(e), 512:768] = pltpu.roll(value, 255, 0).astype(BF16)

    rim = 9 * c
    at_end = (tile == 0) | (tile == NT - 1)
    inside = jnp.logical_not(at_end)
    own = 4 * c
    theirs = 4 - own
    out_row, in_row = 3 * c, 3 - 3 * c

    def finish(r):
        inv = 1.0 / (dens[block(r), :] + 1.0)
        value = acc[block(r), :] * jnp.concatenate([inv, inv], axis=1)
        xbuf[own + r + 1] = value.astype(BF16)

    def hand_over(r):
        e = own + r + 1
        send(None, xbuf.at[e], xbuf.at[e], x_recv.at[r], partner)

    g = 7
    ids = group(g)
    chunk(g, ids, pl.multiple_of(256 * out_row, 256))
    finish(out_row)
    send(inside, xbuf.at[own + out_row + 1], xbuf.at[9 - rim], h_recv, {"tile": tile - 1 + 2 * c})
    chunk(g, ids, pl.multiple_of(256 * in_row, 256))
    finish(in_row)
    hand_over(in_row)
    chunk(g, ids, 256)
    chunk(g, ids, 512)
    finish(1)
    finish(2)
    hand_over(1)
    hand_over(2)
    hand_over(out_row)
    for r in range(4):
        spread(own + r + 1)
    arrived(wbuf.at[pl.ds(0, 144 * (ndp // 2))], f_recv)
    loads[4].wait()

    def conv(r, n):
        pre = jnp.zeros((256 * n, 384), F32)
        for p in range(3):
            pre = pre + jnp.dot(rmat[block(own + r + p, count=n), :], wbuf[768 * p:768 * p + 768, :],
                                preferred_element_type=F32)
        c0 = 0.7978845608028654
        sq = pre * pre
        th = jnp.tanh(c0 * pre * (1.0 + 0.044715 * sq))
        slope = 0.5 * (1.0 + th) + 0.5 * pre * (1.0 - th * th) * (c0 * (1.0 + 3.0 * 0.044715 * sq))
        gp[block(own + r, count=n), :] = (cot[block(r, count=n), :].astype(F32) * slope).astype(BF16)

    def hand_gp(r, n, which):
        rows = block(own + r, count=n)
        send(None, gp.at[rows], gp.at[rows], g_recv.at[which], partner)

    def gp_arrived(n, which):
        arrived(gp.at[pl.ds(0, 256 * n)], g_recv.at[which])

    tn = (((0,), (0,)), ((), ()))

    taps = ((0, 0, 1, 2), (0, 1, 2, 0), (0, 2, 2, 1), (1, 0, 2, 2))

    def outer(row, n, fresh=False):
        right = gp[block(row, count=n), :]

        def put(rows, value):
            if fresh:
                grad[rows, :] = value
            else:
                grad[rows, :] += value

        for i, (p0, q0, p1, q1) in enumerate(taps):
            p = p0 + c * (p1 - p0)
            q = q0 + c * (q1 - q0)
            put(pl.ds(pl.multiple_of(256 * i + 128 * c, 128), 256), lax.dot_general(
                rmat[block(row + p, count=n), block(q)], right, tn, preferred_element_type=F32))
        put(pl.ds(pl.multiple_of(1024 - 1024 * c, 1024), 128), lax.dot_general(
            rmat[block(row + 1, count=n), block(2 + c, 128)], right, tn, preferred_element_type=F32))

    conv(1, 2)
    hand_gp(1, 2, 0)
    outer(own + 1, 2, fresh=True)
    arrived(xbuf.at[0], x_recv.at[out_row])
    spread(theirs + out_row + 1)
    conv(in_row, 1)
    hand_gp(in_row, 1, 1)
    for r in (1, 2):
        arrived(xbuf.at[0], x_recv.at[r])
        spread(theirs + r + 1)
    arrived(xbuf.at[0], x_recv.at[in_row])
    spread(theirs + in_row + 1)
    gp_arrived(2, 0)
    outer(theirs + 1, 2)
    gp_arrived(1, 1)
    outer(jnp.int32(3), 2)

    @pl.when(at_end)
    def _():
        xbuf[rim] = jnp.zeros((256, 256), BF16)

    @pl.when(inside)
    def _():
        arrived(xbuf.at[rim], h_recv)

    spread(rim)
    conv(out_row, 1)
    hand_gp(out_row, 1, 2)
    outer(own + out_row, 1)
    gp_arrived(1, 2)
    outer(theirs + in_row, 1)

    def stacked(value):
        return jnp.concatenate([value[:, 128 * b:128 * b + 128] for b in range(3)], axis=0)

    core0, core1 = c == 0, c == 1

    for j in range(8):
        s2[j, 0:432] = stacked(grad[144 * j:144 * j + 144, :]).astype(BF16)
        s2[j, 432:448] = jnp.zeros((16, 128), BF16)
        send(core0 & (j != y), s2.at[j, pl.ds(0, 432)], ra2.at[y, pl.ds(0, 432)], recvs.at[8],
             at(x, jnp.int32(j), z, c))

        @pl.when(core0 & (j == y))
        def _(j=j):
            ra2[j, 0:432] = s2[j, 0:432]

    for j in range(7):
        send(core1 & (j != z), s2.at[:, pl.ds(64 * j, 64)], rb2.at[z], recvs.at[9], at(x, y, jnp.int32(j), c))

        @pl.when(core1 & (j == z))
        def _(j=j):
            rb2[j] = s2[:, 64 * j:64 * j + 64]

    low_z = z < 7
    both = (c == xhi) & low_z

    @pl.when(core0)
    def _():
        arrived(ra2.at[pl.ds(0, 7), pl.ds(0, 432)], recvs.at[8])
        total = ra2[0, 0:432].astype(F32)
        for i in range(1, 8):
            total = total + ra2[i, 0:432].astype(F32)
        total = jnp.concatenate([total, jnp.zeros((16, 128), F32)], axis=0)
        for j in range(7):
            p3[j] = total[64 * j:64 * j + 64]

    for j in range(7):
        send(core0 & (j != z), p3.at[j], r3.at[z], recvs.at[10], at(x, y, jnp.int32(j), c))

    @pl.when(core1 & low_z)
    def _():
        arrived(rb2.at[pl.ds(0, 7)], recvs.at[9])
        total = rb2[0].astype(F32)
        for i in range(1, 8):
            total = total + rb2[i].astype(F32)
        p3[...] = total

    for j in range(8):
        send(core1 & low_z & (j != y), p3.at[j], r3.at[y], recvs.at[11], at(x, jnp.int32(j), z, c))

    @pl.when(core0 & low_z)
    def _():
        r3[z] = p3[z]
        arrived(r3.at[pl.ds(0, 7)], recvs.at[10])

    @pl.when(core1 & low_z)
    def _():
        r3[y] = p3[y]
        arrived(r3.at[pl.ds(0, 7)], recvs.at[11])

    @pl.when(low_z)
    def _():
        total = r3[0]
        for i in range(1, 8):
            total = total + r3[i]
        q4[...] = total

    for i in range(2):
        xx = 2 * c + i
        send(low_z & (xx != x), q4, r4.at[x], recvs.at[12], at(xx, y, z, c))

    @pl.when(both)
    def _():
        r4[x] = q4[...]

    @pl.when(both)
    def _():
        arrived(r4.at[pl.ds(0, 3)], recvs.at[12])
        f5[z] = ((r4[0] + r4[1]) + (r4[2] + r4[3])).astype(BF16)

    for i in range(8):
        zz = lax.rem(z + i, NZ)
        for cc in ((1 - c,) if i == 0 else (c, 1 - c)):
            send(both, f5.at[z], f5.at[z], recvs.at[13], at(x, y, zz, cc))

    @pl.when(both)
    def _():
        arrived(f5.at[pl.ds(0, 6)], recvs.at[13])

    @pl.when(jnp.logical_not(both))
    def _():
        arrived(f5, recvs.at[13])

    done = f5[...].astype(F32).reshape(448, 128)
    for b in range(3):
        out_ref[:, 128 * b:128 * b + 128] = done[144 * b:144 * b + 144]

    for cond, copy in started:
        under(cond, lambda copy=copy: copy().wait_send())


def local(records, obs_tile, obs_cell, conv_weight, cotangent):
    dma = pltpu.SemaphoreType.DMA
    any_space = pl.BlockSpec(memory_space=pl.ANY)

    def half(*shape):
        return pltpu.VMEM(shape, BF16)

    def full(*shape):
        return pltpu.VMEM(shape, F32)

    def ints(*shape):
        return pltpu.VMEM(shape, jnp.int32)

    return pl.pallas_call(
        fused,
        out_shape=jax.ShapeDtypeStruct((144, 384), F32),
        in_specs=[any_space] * 5,
        out_specs=pl.BlockSpec(memory_space=pltpu.VMEM),
        scratch_shapes=[
            half(1024, 256), ints(1, 1024), ints(1, 1024), half(144, 384), half(1024, 384),
            half(2, 1024, 256), ints(2, 1, 1024), half(2, 1024, 256), half(2, 1024, 256), half(2, 768, 256),
            half(2, 256, 256), ints(2, 1, 1024), ints(2, 1, 1024), ints(2, 1, 1024), ints(2, 1, 1024),
            half(NZ, 4, CAP, 256), ints(NT, 1, CAP), half(NZ, 4, CAP, 256), ints(NT, 1, CAP),
            half(2304, 384), half(10, 256, 256), half(2560, 768), full(1024, 256), full(1024, 128),
            half(2048, 384), full(1152, 384),
            half(8, 448, 128), half(8, 448, 128), half(8, 8, 64, 128), full(8, 64, 128),
            full(8, 64, 128), full(64, 128), full(4, 64, 128), half(7, 64, 128),
            dma((5,)), dma((200,)), dma((2, 12)), dma((2, 4)), dma((NZ,)), dma((NZ,)), dma, dma, dma, dma((4,)), dma((3,)), dma((16,)),
        ],
        compiler_params=pltpu.CompilerParams(
            collective_id=0, has_side_effects=True, vmem_limit_bytes=58 * 1024 * 1024),
    )(records[0], obs_tile.reshape(1, 1024), obs_cell, conv_weight, cotangent.reshape(1024, 384))


def solution(mesh):
    placed = (
        P("dp", "tile", None),
        P("dp", "tile", None),
        P("dp", "tile"),
        P("dp", None),
        P("dp", "tile", None, None),
    )
    return jax.shard_map(
        local, mesh=mesh, in_specs=placed, out_specs=P("dp", None), check_vma=False
    )
```

```python
import jax
import jax.numpy as jnp
from jax import lax
from jax.experimental import pallas as pl
from jax.experimental.pallas import tpu as pltpu
from jax.sharding import PartitionSpec as P

MESH = pl.DeviceIdType.MESH
F32 = jnp.float32
BF16 = jnp.bfloat16
NZ = 8
NY = 8
NT = 32
CAP = 128
FAR = (4, 3, 5, 2, 6, 1, 7)


def remote(src, dst, send, recv, where):
    return pltpu.make_async_remote_copy(
        src_ref=src, dst_ref=dst, send_sem=send, recv_sem=recv,
        device_id=where, device_id_type=MESH,
    )


def fused(rec_hbm, tile_hbm, cell_hbm, w_hbm, cot_hbm, out_ref,
          rec, til, cel, wloc, cot,
          lout, lmeta, h1, h2, h3, h4, m1, m2, m3, m4, sbuf, scell, rbuf, rcell, wbuf, xbuf, rmat, acc, dens, gp, grad,
          s2, ra2, rb2, p3, r3, q4, r4, f5,
          local_sem, sends, ring_recv, meta_recv, rec_recv, cell_recv, w_recv, f_recv, h_recv, x_recv, g_recv, recvs):
    tile = lax.axis_index("tile")
    dp = lax.axis_index("dp")
    z = lax.div(tile, 4)
    kme = lax.rem(tile, 4)
    xlo = lax.div(kme, 2)
    c = lax.rem(tile, 2)
    y = lax.rem(dp, NY)
    xhi = lax.div(dp, NY)
    x = xhi * 2 + xlo
    ndp = 2 * NY
    me = {"tile": tile}

    def at(xx, yy, zz, cc):
        return {"dp": lax.div(xx, 2) * NY + yy, "tile": zz * 4 + lax.rem(xx, 2) * 2 + cc}

    def arrived(ref, sem):
        remote(ref, ref, sem, sem, me).wait_recv()

    started = []

    def under(cond, act):
        if cond is None:
            act()
        else:
            pl.when(cond)(act)

    def send(cond, src, dst, recv, where):
        n = len(started)

        def copy():
            return remote(src, dst, sends.at[n], recv, where)

        started.append((cond, copy))
        under(cond, lambda: copy().start())

    loads = [pltpu.make_async_copy(a, b, local_sem.at[i]) for i, (a, b) in enumerate(
        ((tile_hbm, til), (cell_hbm, cel), (rec_hbm, rec), (w_hbm, wloc), (cot_hbm, cot)))]
    for load in loads:
        load.start()

    flushed = [0]

    def flush(upto):
        for cond, copy in started[flushed[0]:upto]:
            under(cond, lambda copy=copy: copy().wait_send())
        flushed[0] = upto

    barrier = pltpu.get_barrier_semaphore()

    def greet(where):
        pl.semaphore_signal(barrier, inc=1, device_id=where, device_id_type=MESH)

    def greet_dp(i, _):
        greet({"dp": lax.rem(dp + i, ndp)})
        return 0

    for i in FAR:
        greet(at(x, y, lax.rem(z + i, NZ), c))
    for i in range(1, 8):
        greet(at(x, y, lax.rem(z + i, NZ), 1 - c))
    for k in range(1, 4):
        greet({"tile": z * 4 + lax.rem(kme + k, 4)})
    greet({"tile": lax.rem(tile + 1, NT)})
    greet({"tile": lax.rem(tile + NT - 1, NT)})
    lax.fori_loop(1, ndp, greet_dp, 0)
    greet(at(3 - 2 * xhi - xlo, y, z, c))
    loads[0].wait()
    loads[1].wait()

    dest = til[...]
    marks = (lax.broadcasted_iota(jnp.int32, (NT, 1024), 0) == dest).astype(F32)
    upper = (lax.broadcasted_iota(jnp.int32, (256, 256), 0)
             < lax.broadcasted_iota(jnp.int32, (256, 256), 1)).astype(F32).astype(BF16)
    carry = jnp.zeros((NT, 1), F32)
    parts = []
    for i in range(4):
        m = marks[:, 256 * i:256 * i + 256]
        parts.append(jnp.dot(m.astype(BF16), upper, preferred_element_type=F32) + carry)
        carry = carry + jnp.sum(m, axis=1, keepdims=True)
    before = jnp.concatenate(parts, axis=1)
    pos = jnp.sum(before * marks, axis=0, keepdims=True).astype(jnp.int32)
    slot = dest * CAP + pos
    nt = (((1,), (1,)), ((), ()))

    def key(axis, shape, way):
        t = lax.broadcasted_iota(jnp.int32, shape, axis)
        away = jnp.bitwise_and(jnp.right_shift(t, 2) - z, 7)
        if way == 1:
            away = jnp.bitwise_and(8 - away, 7)
        limit = jnp.where(jnp.bitwise_and(t, 1) == way, 4, 3)
        return jnp.where((away >= 1) & (away <= limit), away * NT + t, -1)

    total_b = jnp.broadcast_to(carry, (NT, 128)).astype(BF16)
    spots = []
    for way in range(2):
        down, across = key(0, (NT, NT), way), key(1, (NT, NT), way)
        later = (across > down).astype(F32).astype(BF16)
        offset = jnp.dot(later, total_b, preferred_element_type=F32)[:, 0:1]
        base = jnp.where(key(0, (NT, 1), way) >= 0, 1024.0 - offset - carry, -4096.0)
        spots.append(jnp.sum((base + before) * marks, axis=0, keepdims=True).astype(jnp.int32))
    code = slot + 1
    cell = cel[...]
    traits = jnp.concatenate([
        jnp.right_shift(code, 6).astype(F32), jnp.bitwise_and(code, 63).astype(F32),
        jnp.right_shift(cell, 5).astype(F32), jnp.bitwise_and(cell, 31).astype(F32),
        jnp.zeros((4, 1024), F32)], axis=0).astype(BF16)
    loads[2].wait()

    def own_rows(d):
        return pl.ds(pl.multiple_of(144 * d, 16), 144)

    active = lax.rem(dp + c, 2) == 0
    ahead = ({"tile": lax.rem(tile + 4, NT)}, {"tile": lax.rem(tile + NT - 4, NT)})
    for i in (3, 2, 1, 0):
        for way in range(2):
            rows = pl.ds(256 * i, 256)
            perm = (lax.broadcasted_iota(jnp.int32, (256, 1024), 0) + 256 * i == spots[way]).astype(F32).astype(BF16)
            lout[way, rows] = jnp.dot(perm, rec[...], preferred_element_type=F32).astype(BF16)
            got = lax.dot_general(traits, perm, nt, preferred_element_type=F32)
            number = (got[0:1] * 64.0 + got[1:2]).astype(jnp.int32) - 1
            lmeta[way, :, rows] = number * 1024 + (got[2:3] * 32.0 + got[3:4]).astype(jnp.int32)
            if i == 3 and way == 0:
                pl.semaphore_wait(barrier, 14 + 3 + 2 + ndp - 1 + 1)
            send(None, lout.at[way, rows], h1.at[way, rows], ring_recv.at[way, i], ahead[way])
    for way in range(2):
        send(None, lmeta.at[way], m1.at[way], meta_recv.at[way, 0], ahead[way])
    loads[3].wait()
    for i in range(1, ndp):
        send(active, wloc, wbuf.at[own_rows(dp)], w_recv, {"dp": lax.rem(dp + i, ndp)})
    def share(g, data, number, cell_id):
        length = number.shape[1]
        rel = number - 512 * z
        pick = (lax.broadcasted_iota(jnp.int32, (4 * CAP, length), 0) == rel).astype(F32).astype(BF16)
        packed = jnp.dot(pick, data, preferred_element_type=F32).astype(BF16)
        owner = (lax.broadcasted_iota(jnp.int32, (8, length), 0) == jnp.right_shift(rel, 7)).astype(F32)
        spot = (lax.broadcasted_iota(jnp.int32, (CAP, length), 0) == jnp.bitwise_and(rel, 127)).astype(F32).astype(BF16)
        cell_code = cell_id + 1
        high = jnp.right_shift(cell_code, 5).astype(F32)
        low = jnp.bitwise_and(cell_code, 31).astype(F32)
        chigh = lax.dot_general((owner * high).astype(BF16), spot, nt, preferred_element_type=F32)
        clow = lax.dot_general((owner * low).astype(BF16), spot, nt, preferred_element_type=F32)
        cells = (chigh * 32.0 + clow).astype(jnp.int32) - 1
        for k in range(4):
            scell[4 * g + k] = cells[k:k + 1, :]
            sbuf[g, k] = packed[CAP * k:CAP * k + CAP]
        for k in range(4):
            there = {"tile": z * 4 + k}
            send(k != kme, sbuf.at[g, k], rbuf.at[g, kme], rec_recv.at[g], there)
            send(k != kme, scell.at[4 * g + k], rcell.at[4 * g + kme], cell_recv.at[g], there)
        rbuf[g, kme] = sbuf[g, kme]
        rcell[4 * g + kme] = scell[4 * g + kme]

    def share_list(g, data, meta):
        share(g, data, jnp.right_shift(meta, 10), jnp.bitwise_and(meta, 1023))

    acc[...] = jnp.zeros_like(acc)
    dens[...] = jnp.zeros_like(dens)
    ones = jnp.ones((4 * CAP, 128), BF16)

    def chunk(g, ids, start):
        hit = (lax.broadcasted_iota(jnp.int32, (256, 4 * CAP), 0) + start == ids).astype(F32).astype(BF16)
        rows = pl.ds(start, 256)
        acc[rows, :] += jnp.dot(hit, rbuf[g].reshape(4 * CAP, 256), preferred_element_type=F32)
        dens[rows, :] += jnp.dot(hit, ones, preferred_element_type=F32)

    def group(g):
        arrived(rcell.at[pl.ds(4 * g, 3)], cell_recv.at[g])
        arrived(rbuf.at[g, pl.ds(0, 3)], rec_recv.at[g])
        return jnp.concatenate([rcell[4 * g + k] for k in range(4)], axis=1)

    def into_cells(g):
        ids = group(g)

        def step(r, _):
            chunk(g, ids, pl.multiple_of(r * 256, 256))
            return 0

        lax.fori_loop(0, 4, step, 0)

    share(0, rec[...], slot, cell)

    for way in range(2):
        arrived(m1.at[way], meta_recv.at[way, 0])
        send(None, m1.at[way], m2.at[way], meta_recv.at[way, 1], ahead[way])
    for i in (3, 2, 1, 0):
        rows = pl.ds(256 * i, 256)
        for way in range(2):
            arrived(h1.at[way, rows], ring_recv.at[way, i])
            send(None, h1.at[way, rows], h2.at[way, rows], ring_recv.at[way, 4 + i], ahead[way])
    for way in range(2):
        share_list(1 + way, h1[way], m1[way])
    into_cells(0)

    for way in range(2):
        arrived(m2.at[way], meta_recv.at[way, 1])
        send(None, m2.at[way], m3.at[way], meta_recv.at[way, 2], ahead[way])
    for i in (3, 2, 1, 0):
        rows = pl.ds(256 * i, 256)
        for way in range(2):
            arrived(h2.at[way, rows], ring_recv.at[way, 4 + i])
            if i > 0:
                send(None, h2.at[way, rows], h3.at[way, pl.ds(256 * i - 256, 256)], ring_recv.at[way, 8 + i], ahead[way])
    for way in range(2):
        share_list(3 + way, h2[way], m2[way])
    into_cells(1)
    into_cells(2)

    @pl.when(active)
    def _():
        wbuf[own_rows(dp), :] = wloc[...]
        arrived(wbuf.at[pl.ds(0, 144 * (ndp // 2 - 1))], w_recv)

    @pl.when(jnp.logical_not(active))
    def _():
        arrived(wbuf.at[pl.ds(0, 144 * (ndp // 2))], w_recv)

    partner = at(x, y, z, 1 - c)
    for i in range(ndp // 2):
        rows = own_rows(2 * i + c)
        send(None, wbuf.at[rows], wbuf.at[rows], f_recv, partner)

    for way in range(2):
        arrived(m3.at[way], meta_recv.at[way, 2])
        send(None, m3.at[way], m4.at[way], meta_recv.at[way, 3], ahead[way])
    for i in (3, 2, 1):
        rows = pl.ds(256 * i - 256, 256)
        for way in range(2):
            arrived(h3.at[way, rows], ring_recv.at[way, 8 + i])
            if i == 3:
                send(None, h3.at[way, rows], h4.at[way], ring_recv.at[way, 8], ahead[way])
    for way in range(2):
        share_list(5 + way, h3[way], m3[way][:, 256:1024])
    into_cells(3)
    into_cells(4)
    for way in range(2):
        arrived(m4.at[way], meta_recv.at[way, 3])
        arrived(h4.at[way], ring_recv.at[way, 8])
    share_list(7, h4[...].reshape(512, 256),
               jnp.concatenate([m4[0][:, 768:1024], m4[1][:, 768:1024]], axis=1))
    flush(len(started) - 24)
    into_cells(5)
    into_cells(6)

    def block(n, size=256, count=1):
        return pl.ds(pl.multiple_of(n * size, size), size * count)

    def spread(e):
        value = xbuf[e].astype(F32)
        rmat[block(e), 0:256] = pltpu.roll(value, 1, 0).astype(BF16)
        rmat[block(e), 256:512] = value.astype(BF16)
        rmat[block(e), 512:768] = pltpu.roll(value, 255, 0).astype(BF16)

    rim = 9 * c
    at_end = (tile == 0) | (tile == NT - 1)
    inside = jnp.logical_not(at_end)
    own = 4 * c
    theirs = 4 - own
    out_row, in_row = 3 * c, 3 - 3 * c

    def finish(r):
        inv = 1.0 / (dens[block(r), :] + 1.0)
        value = acc[block(r), :] * jnp.concatenate([inv, inv], axis=1)
        xbuf[own + r + 1] = value.astype(BF16)

    def hand_over(r):
        e = own + r + 1
        send(None, xbuf.at[e], xbuf.at[e], x_recv.at[r], partner)

    g = 7
    ids = group(g)
    chunk(g, ids, pl.multiple_of(256 * out_row, 256))
    finish(out_row)
    send(inside, xbuf.at[own + out_row + 1], xbuf.at[9 - rim], h_recv, {"tile": tile - 1 + 2 * c})
    chunk(g, ids, pl.multiple_of(256 * in_row, 256))
    finish(in_row)
    hand_over(in_row)
    chunk(g, ids, 256)
    chunk(g, ids, 512)
    finish(1)
    finish(2)
    hand_over(1)
    hand_over(2)
    hand_over(out_row)
    for r in range(4):
        spread(own + r + 1)
    arrived(wbuf.at[pl.ds(0, 144 * (ndp // 2))], f_recv)
    loads[4].wait()

    def conv(r, n):
        pre = jnp.zeros((256 * n, 384), F32)
        for p in range(3):
            pre = pre + jnp.dot(rmat[block(own + r + p, count=n), :], wbuf[768 * p:768 * p + 768, :],
                                preferred_element_type=F32)
        c0 = 0.7978845608028654
        sq = pre * pre
        th = jnp.tanh(c0 * pre * (1.0 + 0.044715 * sq))
        slope = 0.5 * (1.0 + th) + 0.5 * pre * (1.0 - th * th) * (c0 * (1.0 + 3.0 * 0.044715 * sq))
        gp[block(own + r, count=n), :] = (cot[block(r, count=n), :].astype(F32) * slope).astype(BF16)

    def hand_gp(r, n, which):
        rows = block(own + r, count=n)
        send(None, gp.at[rows], gp.at[rows], g_recv.at[which], partner)

    def gp_arrived(n, which):
        arrived(gp.at[pl.ds(0, 256 * n)], g_recv.at[which])

    tn = (((0,), (0,)), ((), ()))

    taps = ((0, 0, 1, 2), (0, 1, 2, 0), (0, 2, 2, 1), (1, 0, 2, 2))

    def outer(row, n, fresh=False):
        right = gp[block(row, count=n), :]

        def put(rows, value):
            if fresh:
                grad[rows, :] = value
            else:
                grad[rows, :] += value

        for i, (p0, q0, p1, q1) in enumerate(taps):
            p = p0 + c * (p1 - p0)
            q = q0 + c * (q1 - q0)
            put(pl.ds(pl.multiple_of(256 * i + 128 * c, 128), 256), lax.dot_general(
                rmat[block(row + p, count=n), block(q)], right, tn, preferred_element_type=F32))
        put(pl.ds(pl.multiple_of(1024 - 1024 * c, 1024), 128), lax.dot_general(
            rmat[block(row + 1, count=n), block(2 + c, 128)], right, tn, preferred_element_type=F32))

    conv(1, 2)
    hand_gp(1, 2, 0)
    outer(own + 1, 2, fresh=True)
    arrived(xbuf.at[0], x_recv.at[out_row])
    spread(theirs + out_row + 1)
    conv(in_row, 1)
    hand_gp(in_row, 1, 1)
    for r in (1, 2):
        arrived(xbuf.at[0], x_recv.at[r])
        spread(theirs + r + 1)
    arrived(xbuf.at[0], x_recv.at[in_row])
    spread(theirs + in_row + 1)
    gp_arrived(2, 0)
    outer(theirs + 1, 2)
    gp_arrived(1, 1)
    outer(jnp.int32(3), 2)

    @pl.when(at_end)
    def _():
        xbuf[rim] = jnp.zeros((256, 256), BF16)

    @pl.when(inside)
    def _():
        arrived(xbuf.at[rim], h_recv)

    spread(rim)
    conv(out_row, 1)
    hand_gp(out_row, 1, 2)
    outer(own + out_row, 1)
    gp_arrived(1, 2)
    outer(theirs + in_row, 1)

    def stacked(value):
        return jnp.concatenate([value[:, 128 * b:128 * b + 128] for b in range(3)], axis=0)

    core0, core1 = c == 0, c == 1

    low_z = z < 7
    both = (c == xhi) & low_z
    before_sums = len(started)

    def convert(j):
        s2[j, 0:432] = stacked(grad[own_rows(j), :]).astype(BF16)
        s2[j, 432:448] = jnp.zeros((16, 128), BF16)

    halves = (pl.ds(0, 256), pl.ds(256, 176))

    @pl.when(core0)
    def _():
        for i in FAR:
            convert(lax.rem(y + i, NY))
        convert(y)
        ra2[y] = s2[y]

    for h in range(2):
        for i in FAR:
            j = lax.rem(y + i, NY)
            send(core0, s2.at[j, halves[h]], ra2.at[y, halves[h]], recvs.at[h], at(x, j, z, c))

    for h in range(2):
        fours = pl.ds(4 * h, 4)

        @pl.when(core1)
        def _(h=h, fours=fours):
            for j in range(4 * h, 4 * h + 4):
                convert(j)

            @pl.when(low_z)
            def _():
                for j in range(4 * h, 4 * h + 4):
                    rb2[z, j] = s2[j, block(z, 64)]

        for i in FAR:
            j = lax.rem(z + i, NZ)
            send(core1 & (j < 7), s2.at[fours, block(j, 64)], rb2.at[z, fours], recvs.at[2 + h], at(x, y, j, c))

    flush(before_sums)
    before_second = len(started)
    for h in range(2):
        first_piece, pieces = 4 * h, 4 - h

        @pl.when(core0)
        def _(h=h, first_piece=first_piece, pieces=pieces):
            arrived(ra2.at[pl.ds(0, 7), halves[h]], recvs.at[h])
            n = 256 - 80 * h
            total = ra2[0, 256 * h:256 * h + n].astype(F32)
            for i in range(1, 8):
                total = total + ra2[i, 256 * h:256 * h + n].astype(F32)
            if h == 1:
                total = jnp.concatenate([total, jnp.zeros((16, 128), F32)], axis=0)
            for j in range(pieces):
                p3[first_piece + j] = total[64 * j:64 * j + 64]

        for i in FAR:
            j = lax.rem(z + i, NZ)
            send(core0 & (j >= first_piece) & (j < first_piece + pieces), p3.at[j], r3.at[z], recvs.at[10], at(x, y, j, c))

        @pl.when(core1 & low_z)
        def _(h=h):
            arrived(rb2.at[pl.ds(0, 7), pl.ds(4 * h, 4)], recvs.at[2 + h])
            for j in range(4 * h, 4 * h + 4):
                total = rb2[0, j].astype(F32)
                for i in range(1, 8):
                    total = total + rb2[i, j].astype(F32)
                p3[j] = total

        for i in FAR:
            j = lax.rem(y + i, NY)
            send(core1 & low_z & (lax.div(j, 4) == h), p3.at[j], r3.at[y], recvs.at[11], at(x, j, z, c))

    flush(before_second)

    @pl.when(core0 & low_z)
    def _():
        r3[z] = p3[z]
        arrived(r3.at[pl.ds(0, 7)], recvs.at[10])

    @pl.when(core1 & low_z)
    def _():
        r3[y] = p3[y]
        arrived(r3.at[pl.ds(0, 7)], recvs.at[11])

    @pl.when(low_z)
    def _():
        total = r3[0]
        for i in range(1, 8):
            total = total + r3[i]
        q4[...] = total

    for i in range(2):
        xx = 2 * c + i
        send(low_z & (xx != x), q4, r4.at[x], recvs.at[12], at(xx, y, z, c))

    flush(len(started) - 2)

    @pl.when(both)
    def _():
        r4[x] = q4[...]

    @pl.when(both)
    def _():
        arrived(r4.at[pl.ds(0, 3)], recvs.at[12])
        f5[z] = ((r4[0] + r4[1]) + (r4[2] + r4[3])).astype(BF16)

    for i in FAR + (0,):
        zz = lax.rem(z + i, NZ)
        for cc in ((1 - c,) if i == 0 else (c, 1 - c)):
            send(both, f5.at[z], f5.at[z], recvs.at[13], at(x, y, zz, cc))

    flush(len(started) - 15)

    @pl.when(both)
    def _():
        arrived(f5.at[pl.ds(0, 6)], recvs.at[13])

    @pl.when(jnp.logical_not(both))
    def _():
        arrived(f5, recvs.at[13])

    done = f5[...].astype(F32).reshape(448, 128)
    for b in range(3):
        out_ref[:, 128 * b:128 * b + 128] = done[144 * b:144 * b + 144]

    flush(len(started))


def local(records, obs_tile, obs_cell, conv_weight, cotangent):
    dma = pltpu.SemaphoreType.DMA
    any_space = pl.BlockSpec(memory_space=pl.ANY)

    def half(*shape):
        return pltpu.VMEM(shape, BF16)

    def full(*shape):
        return pltpu.VMEM(shape, F32)

    def ints(*shape):
        return pltpu.VMEM(shape, jnp.int32)

    return pl.pallas_call(
        fused,
        out_shape=jax.ShapeDtypeStruct((144, 384), F32),
        in_specs=[any_space] * 5,
        out_specs=pl.BlockSpec(memory_space=pltpu.VMEM),
        scratch_shapes=[
            half(1024, 256), ints(1, 1024), ints(1, 1024), half(144, 384), half(1024, 384),
            half(2, 1024, 256), ints(2, 1, 1024), half(2, 1024, 256), half(2, 1024, 256), half(2, 768, 256),
            half(2, 256, 256), ints(2, 1, 1024), ints(2, 1, 1024), ints(2, 1, 1024), ints(2, 1, 1024),
            half(NZ, 4, CAP, 256), ints(NT, 1, CAP), half(NZ, 4, CAP, 256), ints(NT, 1, CAP),
            half(2304, 384), half(10, 256, 256), half(2560, 768), full(1024, 256), full(1024, 128),
            half(2048, 384), full(1152, 384),
            half(8, 448, 128), half(8, 448, 128), half(8, 8, 64, 128), full(8, 64, 128),
            full(8, 64, 128), full(64, 128), full(4, 64, 128), half(7, 64, 128),
            dma((5,)), dma((240,)), dma((2, 12)), dma((2, 4)), dma((NZ,)), dma((NZ,)), dma, dma, dma, dma((4,)), dma((3,)), dma((16,)),
        ],
        compiler_params=pltpu.CompilerParams(
            collective_id=0, has_side_effects=True, vmem_limit_bytes=58 * 1024 * 1024),
    )(records[0], obs_tile.reshape(1, 1024), obs_cell, conv_weight, cotangent.reshape(1024, 384))


def solution(mesh):
    placed = (
        P("dp", "tile", None),
        P("dp", "tile", None),
        P("dp", "tile"),
        P("dp", None),
        P("dp", "tile", None, None),
    )
    return jax.shard_map(
        local, mesh=mesh, in_specs=placed, out_specs=P("dp", None), check_vma=False
    )
```

```python
import jax
import jax.numpy as jnp
from jax import lax
from jax.experimental import pallas as pl
from jax.experimental.pallas import tpu as pltpu
from jax.sharding import PartitionSpec as P

MESH = pl.DeviceIdType.MESH
F32 = jnp.float32
BF16 = jnp.bfloat16
NZ = 8
NY = 8
NT = 32
CAP = 128
FAR = (4, 3, 5, 2, 6, 1, 7)


def remote(src, dst, send, recv, where):
    return pltpu.make_async_remote_copy(
        src_ref=src, dst_ref=dst, send_sem=send, recv_sem=recv,
        device_id=where, device_id_type=MESH,
    )


def fused(rec_hbm, tile_hbm, cell_hbm, w_hbm, cot_hbm, out_ref,
          rec, til, cel, wloc, cot,
          lout, lmeta, h1, h2, h3, h4, m1, m2, m3, m4, sbuf, scell, rbuf, rcell, wbuf, xbuf, rmat, acc, dens, gp, grad,
          s2, ra2, rb2, p3, r3, q4, r4, f5,
          local_sem, news, sends, ring_recv, meta_recv, rec_recv, cell_recv, w_recv, f_recv, h_recv, x_recv, g_recv, recvs):
    tile = lax.axis_index("tile")
    dp = lax.axis_index("dp")
    z = lax.div(tile, 4)
    kme = lax.rem(tile, 4)
    xlo = lax.div(kme, 2)
    c = lax.rem(tile, 2)
    y = lax.rem(dp, NY)
    xhi = lax.div(dp, NY)
    x = xhi * 2 + xlo
    ndp = 2 * NY
    me = {"tile": tile}

    def at(xx, yy, zz, cc):
        return {"dp": lax.div(xx, 2) * NY + yy, "tile": zz * 4 + lax.rem(xx, 2) * 2 + cc}

    def arrived(ref, sem):
        remote(ref, ref, sem, sem, me).wait_recv()

    started = []

    def under(cond, act):
        if cond is None:
            act()
        else:
            pl.when(cond)(act)

    def send(cond, src, dst, recv, where):
        n = len(started)

        def copy():
            return remote(src, dst, sends.at[n], recv, where)

        started.append((cond, copy))
        under(cond, lambda: copy().start())

    loads = [pltpu.make_async_copy(a, b, local_sem.at[i]) for i, (a, b) in enumerate(
        ((tile_hbm, til), (cell_hbm, cel), (rec_hbm, rec), (w_hbm, wloc), (cot_hbm, cot)))]
    for load in loads:
        load.start()

    flushed = [0]

    def flush(upto):
        for cond, copy in started[flushed[0]:upto]:
            under(cond, lambda copy=copy: copy().wait_send())
        flushed[0] = upto

    barrier = pltpu.get_barrier_semaphore()

    def greet(where):
        pl.semaphore_signal(barrier, inc=1, device_id=where, device_id_type=MESH)

    ahead = ({"tile": lax.rem(tile + 4, NT)}, {"tile": lax.rem(tile + NT - 4, NT)})
    beside = (at(x, lax.rem(y + 1, NY), z, c), at(x, lax.rem(y + NY - 1, NY), z, c))
    for where in ahead + beside:
        greet(where)
    for k in range(1, 4):
        greet({"tile": z * 4 + lax.rem(kme + k, 4)})
    greet(at(lax.rem(x + 2, 4), y, z, c))
    greet(at(3 - x, y, z, c))

    def tell(n):
        for where in ahead + beside:
            pl.semaphore_signal(news.at[n], inc=1, device_id=where, device_id_type=MESH)

    def hear(n):
        pl.semaphore_wait(news.at[n], 4)

    loads[0].wait()
    loads[1].wait()

    dest = til[...]
    marks = (lax.broadcasted_iota(jnp.int32, (NT, 1024), 0) == dest).astype(F32)
    upper = (lax.broadcasted_iota(jnp.int32, (256, 256), 0)
             < lax.broadcasted_iota(jnp.int32, (256, 256), 1)).astype(F32).astype(BF16)
    carry = jnp.zeros((NT, 1), F32)
    parts = []
    for i in range(4):
        m = marks[:, 256 * i:256 * i + 256]
        parts.append(jnp.dot(m.astype(BF16), upper, preferred_element_type=F32) + carry)
        carry = carry + jnp.sum(m, axis=1, keepdims=True)
    before = jnp.concatenate(parts, axis=1)
    pos = jnp.sum(before * marks, axis=0, keepdims=True).astype(jnp.int32)
    slot = dest * CAP + pos
    nt = (((1,), (1,)), ((), ()))

    def key(axis, shape, way):
        t = lax.broadcasted_iota(jnp.int32, shape, axis)
        away = jnp.bitwise_and(jnp.right_shift(t, 2) - z, 7)
        if way == 1:
            away = jnp.bitwise_and(8 - away, 7)
        limit = jnp.where(jnp.bitwise_and(t, 1) == way, 4, 3)
        return jnp.where((away >= 1) & (away <= limit), away * NT + t, -1)

    total_b = jnp.broadcast_to(carry, (NT, 128)).astype(BF16)
    spots = []
    for way in range(2):
        down, across = key(0, (NT, NT), way), key(1, (NT, NT), way)
        later = (across > down).astype(F32).astype(BF16)
        offset = jnp.dot(later, total_b, preferred_element_type=F32)[:, 0:1]
        base = jnp.where(key(0, (NT, 1), way) >= 0, 1024.0 - offset - carry, -4096.0)
        spots.append(jnp.sum((base + before) * marks, axis=0, keepdims=True).astype(jnp.int32))
    code = slot + 1
    cell = cel[...]
    traits = jnp.concatenate([
        jnp.right_shift(code, 6).astype(F32), jnp.bitwise_and(code, 63).astype(F32),
        jnp.right_shift(cell, 5).astype(F32), jnp.bitwise_and(cell, 31).astype(F32),
        jnp.zeros((4, 1024), F32)], axis=0).astype(BF16)
    loads[2].wait()

    def own_rows(d):
        return pl.ds(pl.multiple_of(144 * d, 16), 144)

    active = lax.rem(dp + c, 2) == 0
    for i in (3, 2, 1, 0):
        for way in range(2):
            rows = pl.ds(256 * i, 256)
            perm = (lax.broadcasted_iota(jnp.int32, (256, 1024), 0) + 256 * i == spots[way]).astype(F32).astype(BF16)
            lout[way, rows] = jnp.dot(perm, rec[...], preferred_element_type=F32).astype(BF16)
            got = lax.dot_general(traits, perm, nt, preferred_element_type=F32)
            number = (got[0:1] * 64.0 + got[1:2]).astype(jnp.int32) - 1
            lmeta[way, :, rows] = number * 1024 + (got[2:3] * 32.0 + got[3:4]).astype(jnp.int32)
            if i == 3 and way == 0:
                pl.semaphore_wait(barrier, 9)
            send(None, lout.at[way, rows], h1.at[way, rows], ring_recv.at[way, i], ahead[way])
    for way in range(2):
        send(None, lmeta.at[way], m1.at[way], meta_recv.at[way, 0], ahead[way])
    loads[3].wait()
    tell(0)
    def share(g, data, number, cell_id):
        length = number.shape[1]
        rel = number - 512 * z
        pick = (lax.broadcasted_iota(jnp.int32, (4 * CAP, length), 0) == rel).astype(F32).astype(BF16)
        packed = jnp.dot(pick, data, preferred_element_type=F32).astype(BF16)
        owner = (lax.broadcasted_iota(jnp.int32, (8, length), 0) == jnp.right_shift(rel, 7)).astype(F32)
        spot = (lax.broadcasted_iota(jnp.int32, (CAP, length), 0) == jnp.bitwise_and(rel, 127)).astype(F32).astype(BF16)
        cell_code = cell_id + 1
        high = jnp.right_shift(cell_code, 5).astype(F32)
        low = jnp.bitwise_and(cell_code, 31).astype(F32)
        chigh = lax.dot_general((owner * high).astype(BF16), spot, nt, preferred_element_type=F32)
        clow = lax.dot_general((owner * low).astype(BF16), spot, nt, preferred_element_type=F32)
        cells = (chigh * 32.0 + clow).astype(jnp.int32) - 1
        for k in range(4):
            scell[4 * g + k] = cells[k:k + 1, :]
            sbuf[g, k] = packed[CAP * k:CAP * k + CAP]
        for k in range(4):
            there = {"tile": z * 4 + k}
            send(k != kme, sbuf.at[g, k], rbuf.at[g, kme], rec_recv.at[g], there)
            send(k != kme, scell.at[4 * g + k], rcell.at[4 * g + kme], cell_recv.at[g], there)
        rbuf[g, kme] = sbuf[g, kme]
        rcell[4 * g + kme] = scell[4 * g + kme]

    def share_list(g, data, meta):
        share(g, data, jnp.right_shift(meta, 10), jnp.bitwise_and(meta, 1023))

    acc[...] = jnp.zeros_like(acc)
    dens[...] = jnp.zeros_like(dens)
    ones = jnp.ones((4 * CAP, 128), BF16)

    def chunk(g, ids, start):
        hit = (lax.broadcasted_iota(jnp.int32, (256, 4 * CAP), 0) + start == ids).astype(F32).astype(BF16)
        rows = pl.ds(start, 256)
        acc[rows, :] += jnp.dot(hit, rbuf[g].reshape(4 * CAP, 256), preferred_element_type=F32)
        dens[rows, :] += jnp.dot(hit, ones, preferred_element_type=F32)

    def group(g):
        arrived(rcell.at[pl.ds(4 * g, 3)], cell_recv.at[g])
        arrived(rbuf.at[g, pl.ds(0, 3)], rec_recv.at[g])
        return jnp.concatenate([rcell[4 * g + k] for k in range(4)], axis=1)

    def into_cells(g):
        ids = group(g)

        def step(r, _):
            chunk(g, ids, pl.multiple_of(r * 256, 256))
            return 0

        lax.fori_loop(0, 4, step, 0)

    share(0, rec[...], slot, cell)

    for way in range(2):
        arrived(m1.at[way], meta_recv.at[way, 0])
        send(None, m1.at[way], m2.at[way], meta_recv.at[way, 1], ahead[way])
    for i in (3, 2, 1, 0):
        rows = pl.ds(256 * i, 256)
        for way in range(2):
            arrived(h1.at[way, rows], ring_recv.at[way, i])
            send(None, h1.at[way, rows], h2.at[way, rows], ring_recv.at[way, 4 + i], ahead[way])
        hear(3 - i)
        if i > 0:
            tell(4 - i)
    for i in range(1, ndp):
        send(active, wloc, wbuf.at[own_rows(dp)], w_recv, {"dp": lax.rem(dp + i, ndp)})
    for way in range(2):
        share_list(1 + way, h1[way], m1[way])
    into_cells(0)

    for way in range(2):
        arrived(m2.at[way], meta_recv.at[way, 1])
        send(None, m2.at[way], m3.at[way], meta_recv.at[way, 2], ahead[way])
    for i in (3, 2, 1, 0):
        rows = pl.ds(256 * i, 256)
        for way in range(2):
            arrived(h2.at[way, rows], ring_recv.at[way, 4 + i])
            if i > 0:
                send(None, h2.at[way, rows], h3.at[way, pl.ds(256 * i - 256, 256)], ring_recv.at[way, 8 + i], ahead[way])
    for way in range(2):
        share_list(3 + way, h2[way], m2[way])
    into_cells(1)
    into_cells(2)

    for way in range(2):
        arrived(m3.at[way], meta_recv.at[way, 2])
        send(None, m3.at[way], m4.at[way], meta_recv.at[way, 3], ahead[way])
    for i in (3, 2, 1):
        rows = pl.ds(256 * i - 256, 256)
        for way in range(2):
            arrived(h3.at[way, rows], ring_recv.at[way, 8 + i])
            if i == 3:
                send(None, h3.at[way, rows], h4.at[way], ring_recv.at[way, 8], ahead[way])
    for way in range(2):
        share_list(5 + way, h3[way], m3[way][:, 256:1024])
    into_cells(3)
    into_cells(4)
    for way in range(2):
        arrived(m4.at[way], meta_recv.at[way, 3])
        arrived(h4.at[way], ring_recv.at[way, 8])
    share_list(7, h4[...].reshape(512, 256),
               jnp.concatenate([m4[0][:, 768:1024], m4[1][:, 768:1024]], axis=1))
    flush(len(started) - 24)
    into_cells(5)
    into_cells(6)

    @pl.when(active)
    def _():
        wbuf[own_rows(dp), :] = wloc[...]
        arrived(wbuf.at[pl.ds(0, 144 * (ndp // 2 - 1))], w_recv)

    @pl.when(jnp.logical_not(active))
    def _():
        arrived(wbuf.at[pl.ds(0, 144 * (ndp // 2))], w_recv)

    partner = at(x, y, z, 1 - c)
    for i in range(ndp // 2):
        rows = own_rows(2 * i + c)
        send(None, wbuf.at[rows], wbuf.at[rows], f_recv, partner)


    def block(n, size=256, count=1):
        return pl.ds(pl.multiple_of(n * size, size), size * count)

    def spread(e):
        value = xbuf[e].astype(F32)
        rmat[block(e), 0:256] = pltpu.roll(value, 1, 0).astype(BF16)
        rmat[block(e), 256:512] = value.astype(BF16)
        rmat[block(e), 512:768] = pltpu.roll(value, 255, 0).astype(BF16)

    rim = 9 * c
    at_end = (tile == 0) | (tile == NT - 1)
    inside = jnp.logical_not(at_end)
    own = 4 * c
    theirs = 4 - own
    out_row, in_row = 3 * c, 3 - 3 * c

    def finish(r):
        inv = 1.0 / (dens[block(r), :] + 1.0)
        value = acc[block(r), :] * jnp.concatenate([inv, inv], axis=1)
        xbuf[own + r + 1] = value.astype(BF16)

    def hand_over(r):
        e = own + r + 1
        send(None, xbuf.at[e], xbuf.at[e], x_recv.at[r], partner)

    g = 7
    ids = group(g)
    chunk(g, ids, pl.multiple_of(256 * out_row, 256))
    finish(out_row)
    send(inside, xbuf.at[own + out_row + 1], xbuf.at[9 - rim], h_recv, {"tile": tile - 1 + 2 * c})
    chunk(g, ids, pl.multiple_of(256 * in_row, 256))
    finish(in_row)
    hand_over(in_row)
    chunk(g, ids, 256)
    chunk(g, ids, 512)
    finish(1)
    finish(2)
    hand_over(1)
    hand_over(2)
    hand_over(out_row)
    for r in range(4):
        spread(own + r + 1)
    arrived(wbuf.at[pl.ds(0, 144 * (ndp // 2))], f_recv)
    loads[4].wait()

    def conv(r, n):
        pre = jnp.zeros((256 * n, 384), F32)
        for p in range(3):
            pre = pre + jnp.dot(rmat[block(own + r + p, count=n), :], wbuf[768 * p:768 * p + 768, :],
                                preferred_element_type=F32)
        c0 = 0.7978845608028654
        sq = pre * pre
        th = jnp.tanh(c0 * pre * (1.0 + 0.044715 * sq))
        slope = 0.5 * (1.0 + th) + 0.5 * pre * (1.0 - th * th) * (c0 * (1.0 + 3.0 * 0.044715 * sq))
        gp[block(own + r, count=n), :] = (cot[block(r, count=n), :].astype(F32) * slope).astype(BF16)

    def hand_gp(r, n, which):
        rows = block(own + r, count=n)
        send(None, gp.at[rows], gp.at[rows], g_recv.at[which], partner)

    def gp_arrived(n, which):
        arrived(gp.at[pl.ds(0, 256 * n)], g_recv.at[which])

    tn = (((0,), (0,)), ((), ()))

    taps = ((0, 0, 1, 2), (0, 1, 2, 0), (0, 2, 2, 1), (1, 0, 2, 2))

    def outer(row, n, fresh=False):
        right = gp[block(row, count=n), :]

        def put(rows, value):
            if fresh:
                grad[rows, :] = value
            else:
                grad[rows, :] += value

        for i, (p0, q0, p1, q1) in enumerate(taps):
            p = p0 + c * (p1 - p0)
            q = q0 + c * (q1 - q0)
            put(pl.ds(pl.multiple_of(256 * i + 128 * c, 128), 256), lax.dot_general(
                rmat[block(row + p, count=n), block(q)], right, tn, preferred_element_type=F32))
        put(pl.ds(pl.multiple_of(1024 - 1024 * c, 1024), 128), lax.dot_general(
            rmat[block(row + 1, count=n), block(2 + c, 128)], right, tn, preferred_element_type=F32))

    conv(1, 2)
    hand_gp(1, 2, 0)
    outer(own + 1, 2, fresh=True)
    arrived(xbuf.at[0], x_recv.at[out_row])
    spread(theirs + out_row + 1)
    conv(in_row, 1)
    hand_gp(in_row, 1, 1)
    for r in (1, 2):
        arrived(xbuf.at[0], x_recv.at[r])
        spread(theirs + r + 1)
    arrived(xbuf.at[0], x_recv.at[in_row])
    spread(theirs + in_row + 1)
    gp_arrived(2, 0)
    outer(theirs + 1, 2)
    gp_arrived(1, 1)
    outer(jnp.int32(3), 2)

    @pl.when(at_end)
    def _():
        xbuf[rim] = jnp.zeros((256, 256), BF16)

    @pl.when(inside)
    def _():
        arrived(xbuf.at[rim], h_recv)

    spread(rim)
    conv(out_row, 1)
    hand_gp(out_row, 1, 2)
    outer(own + out_row, 1)
    gp_arrived(1, 2)
    outer(theirs + in_row, 1)

    def stacked(value):
        return jnp.concatenate([value[:, 128 * b:128 * b + 128] for b in range(3)], axis=0)

    core0, core1 = c == 0, c == 1

    low_z = z < 7
    both = (c == xhi) & low_z
    before_sums = len(started)

    def convert(j):
        s2[j, 0:432] = stacked(grad[own_rows(j), :]).astype(BF16)
        s2[j, 432:448] = jnp.zeros((16, 128), BF16)

    halves = (pl.ds(0, 256), pl.ds(256, 176))

    @pl.when(core0)
    def _():
        for i in FAR:
            convert(lax.rem(y + i, NY))
        convert(y)
        ra2[y] = s2[y]

    for h in range(2):
        for i in FAR:
            j = lax.rem(y + i, NY)
            send(core0, s2.at[j, halves[h]], ra2.at[y, halves[h]], recvs.at[h], at(x, j, z, c))

    for h in range(2):
        fours = pl.ds(4 * h, 4)

        @pl.when(core1)
        def _(h=h, fours=fours):
            for j in range(4 * h, 4 * h + 4):
                convert(j)

            @pl.when(low_z)
            def _():
                for j in range(4 * h, 4 * h + 4):
                    rb2[z, j] = s2[j, block(z, 64)]

        for i in FAR:
            j = lax.rem(z + i, NZ)
            send(core1 & (j < 7), s2.at[fours, block(j, 64)], rb2.at[z, fours], recvs.at[2 + h], at(x, y, j, c))

    flush(before_sums)
    before_second = len(started)
    for h in range(2):
        first_piece, pieces = 4 * h, 4 - h

        @pl.when(core0)
        def _(h=h, first_piece=first_piece, pieces=pieces):
            arrived(ra2.at[pl.ds(0, 7), halves[h]], recvs.at[h])
            n = 256 - 80 * h
            total = ra2[0, 256 * h:256 * h + n].astype(F32)
            for i in range(1, 8):
                total = total + ra2[i, 256 * h:256 * h + n].astype(F32)
            if h == 1:
                total = jnp.concatenate([total, jnp.zeros((16, 128), F32)], axis=0)
            for j in range(pieces):
                p3[first_piece + j] = total[64 * j:64 * j + 64]

        for i in FAR:
            j = lax.rem(z + i, NZ)
            send(core0 & (j >= first_piece) & (j < first_piece + pieces), p3.at[j], r3.at[z], recvs.at[10], at(x, y, j, c))

        @pl.when(core1 & low_z)
        def _(h=h):
            arrived(rb2.at[pl.ds(0, 7), pl.ds(4 * h, 4)], recvs.at[2 + h])
            for j in range(4 * h, 4 * h + 4):
                total = rb2[0, j].astype(F32)
                for i in range(1, 8):
                    total = total + rb2[i, j].astype(F32)
                p3[j] = total

        for i in FAR:
            j = lax.rem(y + i, NY)
            send(core1 & low_z & (lax.div(j, 4) == h), p3.at[j], r3.at[y], recvs.at[11], at(x, j, z, c))

    flush(before_second)

    @pl.when(core0 & low_z)
    def _():
        r3[z] = p3[z]
        arrived(r3.at[pl.ds(0, 7)], recvs.at[10])

    @pl.when(core1 & low_z)
    def _():
        r3[y] = p3[y]
        arrived(r3.at[pl.ds(0, 7)], recvs.at[11])

    @pl.when(low_z)
    def _():
        total = r3[0]
        for i in range(1, 8):
            total = total + r3[i]
        q4[...] = total

    for i in range(2):
        xx = 2 * c + i
        send(low_z & (xx != x), q4, r4.at[x], recvs.at[12], at(xx, y, z, c))

    flush(len(started) - 2)

    @pl.when(both)
    def _():
        r4[x] = q4[...]

    @pl.when(both)
    def _():
        arrived(r4.at[pl.ds(0, 3)], recvs.at[12])
        f5[z] = ((r4[0] + r4[1]) + (r4[2] + r4[3])).astype(BF16)

    for i in FAR + (0,):
        zz = lax.rem(z + i, NZ)
        for cc in ((1 - c,) if i == 0 else (c, 1 - c)):
            send(both, f5.at[z], f5.at[z], recvs.at[13], at(x, y, zz, cc))

    flush(len(started) - 15)

    @pl.when(both)
    def _():
        arrived(f5.at[pl.ds(0, 6)], recvs.at[13])

    @pl.when(jnp.logical_not(both))
    def _():
        arrived(f5, recvs.at[13])

    done = f5[...].astype(F32).reshape(448, 128)
    for b in range(3):
        out_ref[:, 128 * b:128 * b + 128] = done[144 * b:144 * b + 144]

    flush(len(started))


def local(records, obs_tile, obs_cell, conv_weight, cotangent):
    dma = pltpu.SemaphoreType.DMA
    any_space = pl.BlockSpec(memory_space=pl.ANY)

    def half(*shape):
        return pltpu.VMEM(shape, BF16)

    def full(*shape):
        return pltpu.VMEM(shape, F32)

    def ints(*shape):
        return pltpu.VMEM(shape, jnp.int32)

    return pl.pallas_call(
        fused,
        out_shape=jax.ShapeDtypeStruct((144, 384), F32),
        in_specs=[any_space] * 5,
        out_specs=pl.BlockSpec(memory_space=pltpu.VMEM),
        scratch_shapes=[
            half(1024, 256), ints(1, 1024), ints(1, 1024), half(144, 384), half(1024, 384),
            half(2, 1024, 256), ints(2, 1, 1024), half(2, 1024, 256), half(2, 1024, 256), half(2, 768, 256),
            half(2, 256, 256), ints(2, 1, 1024), ints(2, 1, 1024), ints(2, 1, 1024), ints(2, 1, 1024),
            half(NZ, 4, CAP, 256), ints(NT, 1, CAP), half(NZ, 4, CAP, 256), ints(NT, 1, CAP),
            half(2304, 384), half(10, 256, 256), half(2560, 768), full(1024, 256), full(1024, 128),
            half(2048, 384), full(1152, 384),
            half(8, 448, 128), half(8, 448, 128), half(8, 8, 64, 128), full(8, 64, 128),
            full(8, 64, 128), full(64, 128), full(4, 64, 128), half(7, 64, 128),
            dma((5,)), pltpu.SemaphoreType.REGULAR((4,)), dma((240,)), dma((2, 12)), dma((2, 4)), dma((NZ,)), dma((NZ,)), dma, dma, dma, dma((4,)), dma((3,)), dma((16,)),
        ],
        compiler_params=pltpu.CompilerParams(
            collective_id=0, has_side_effects=True, vmem_limit_bytes=58 * 1024 * 1024),
    )(records[0], obs_tile.reshape(1, 1024), obs_cell, conv_weight, cotangent.reshape(1024, 384))


def solution(mesh):
    placed = (
        P("dp", "tile", None),
        P("dp", "tile", None),
        P("dp", "tile"),
        P("dp", None),
        P("dp", "tile", None, None),
    )
    return jax.shard_map(
        local, mesh=mesh, in_specs=placed, out_specs=P("dp", None), check_vma=False
    )
```

```python
import jax
import jax.numpy as jnp
from jax import lax
from jax.experimental import pallas as pl
from jax.experimental.pallas import tpu as pltpu
from jax.sharding import PartitionSpec as P

MESH = pl.DeviceIdType.MESH
F32 = jnp.float32
BF16 = jnp.bfloat16
NZ = 8
NY = 8
NT = 32
CAP = 128
FAR = (4, 3, 5, 2, 6, 1, 7)


def remote(src, dst, send, recv, where):
    return pltpu.make_async_remote_copy(
        src_ref=src, dst_ref=dst, send_sem=send, recv_sem=recv,
        device_id=where, device_id_type=MESH,
    )


def fused(rec_hbm, tile_hbm, cell_hbm, w_hbm, cot_hbm, out_ref,
          rec, til, cel, wloc, cot,
          lout, lmeta, h1, h2, h3, h4, m1, m2, m3, m4, sbuf, scell, rbuf, rcell, wbuf, xbuf, rmat, acc, dens, gp, grad,
          s2, ra2, rb2, p3, r3, q4, r4, f5,
          local_sem, news, sends, ring_recv, meta_recv, rec_recv, cell_recv, w_recv, f_recv, h_recv, x_recv, g_recv, recvs):
    tile = lax.axis_index("tile")
    dp = lax.axis_index("dp")
    z = lax.div(tile, 4)
    kme = lax.rem(tile, 4)
    xlo = lax.div(kme, 2)
    c = lax.rem(tile, 2)
    y = lax.rem(dp, NY)
    xhi = lax.div(dp, NY)
    x = xhi * 2 + xlo
    ndp = 2 * NY
    me = {"tile": tile}

    def at(xx, yy, zz, cc):
        return {"dp": lax.div(xx, 2) * NY + yy, "tile": zz * 4 + lax.rem(xx, 2) * 2 + cc}

    def arrived(ref, sem):
        remote(ref, ref, sem, sem, me).wait_recv()

    started = []

    def under(cond, act):
        if cond is None:
            act()
        else:
            pl.when(cond)(act)

    def send(cond, src, dst, recv, where):
        n = len(started)

        def copy():
            return remote(src, dst, sends.at[n], recv, where)

        started.append((cond, copy))
        under(cond, lambda: copy().start())

    loads = [pltpu.make_async_copy(a, b, local_sem.at[i]) for i, (a, b) in enumerate(
        ((tile_hbm, til), (cell_hbm, cel), (rec_hbm, rec), (w_hbm, wloc), (cot_hbm, cot)))]
    for load in loads:
        load.start()

    flushed = [0]

    def flush(upto):
        for cond, copy in started[flushed[0]:upto]:
            under(cond, lambda copy=copy: copy().wait_send())
        flushed[0] = upto

    barrier = pltpu.get_barrier_semaphore()

    def greet(where):
        pl.semaphore_signal(barrier, inc=1, device_id=where, device_id_type=MESH)

    ahead = ({"tile": lax.rem(tile + 4, NT)}, {"tile": lax.rem(tile + NT - 4, NT)})
    beside = (at(x, lax.rem(y + 1, NY), z, c), at(x, lax.rem(y + NY - 1, NY), z, c))
    for where in ahead + beside:
        greet(where)
    for k in range(1, 4):
        greet({"tile": z * 4 + lax.rem(kme + k, 4)})
    greet(at(lax.rem(x + 2, 4), y, z, c))
    greet(at(3 - x, y, z, c))

    def tell(n):
        for where in ahead + beside:
            pl.semaphore_signal(news.at[n], inc=1, device_id=where, device_id_type=MESH)

    def hear(n):
        pl.semaphore_wait(news.at[n], 4)

    loads[0].wait()
    loads[1].wait()

    dest = til[...]
    marks = (lax.broadcasted_iota(jnp.int32, (NT, 1024), 0) == dest).astype(F32)
    upper = (lax.broadcasted_iota(jnp.int32, (256, 256), 0)
             < lax.broadcasted_iota(jnp.int32, (256, 256), 1)).astype(F32).astype(BF16)
    carry = jnp.zeros((NT, 1), F32)
    parts = []
    for i in range(4):
        m = marks[:, 256 * i:256 * i + 256]
        parts.append(jnp.dot(m.astype(BF16), upper, preferred_element_type=F32) + carry)
        carry = carry + jnp.sum(m, axis=1, keepdims=True)
    before = jnp.concatenate(parts, axis=1)
    pos = jnp.sum(before * marks, axis=0, keepdims=True).astype(jnp.int32)
    slot = dest * CAP + pos
    nt = (((1,), (1,)), ((), ()))

    def key(axis, shape, way):
        t = lax.broadcasted_iota(jnp.int32, shape, axis)
        away = jnp.bitwise_and(jnp.right_shift(t, 2) - z, 7)
        if way == 1:
            away = jnp.bitwise_and(8 - away, 7)
        limit = jnp.where(jnp.bitwise_and(t, 1) == way, 4, 3)
        return jnp.where((away >= 1) & (away <= limit), away * NT + t, -1)

    total_b = jnp.broadcast_to(carry, (NT, 128)).astype(BF16)
    spots = []
    for way in range(2):
        down, across = key(0, (NT, NT), way), key(1, (NT, NT), way)
        later = (across > down).astype(F32).astype(BF16)
        offset = jnp.dot(later, total_b, preferred_element_type=F32)[:, 0:1]
        base = jnp.where(key(0, (NT, 1), way) >= 0, 1024.0 - offset - carry, -4096.0)
        spots.append(jnp.sum((base + before) * marks, axis=0, keepdims=True).astype(jnp.int32))
    code = slot + 1
    cell = cel[...]
    traits = jnp.concatenate([
        jnp.right_shift(code, 6).astype(F32), jnp.bitwise_and(code, 63).astype(F32),
        jnp.right_shift(cell, 5).astype(F32), jnp.bitwise_and(cell, 31).astype(F32),
        jnp.zeros((4, 1024), F32)], axis=0).astype(BF16)
    loads[2].wait()

    def own_rows(d):
        return pl.ds(pl.multiple_of(144 * d, 16), 144)

    active = lax.rem(dp + c, 2) == 0
    for i in (3, 2, 1, 0):
        for way in range(2):
            rows = pl.ds(256 * i, 256)
            perm = (lax.broadcasted_iota(jnp.int32, (256, 1024), 0) + 256 * i == spots[way]).astype(F32).astype(BF16)
            lout[way, rows] = jnp.dot(perm, rec[...], preferred_element_type=F32).astype(BF16)
            got = lax.dot_general(traits, perm, nt, preferred_element_type=F32)
            number = (got[0:1] * 64.0 + got[1:2]).astype(jnp.int32) - 1
            lmeta[way, :, rows] = number * 1024 + (got[2:3] * 32.0 + got[3:4]).astype(jnp.int32)
            if i == 3 and way == 0:
                pl.semaphore_wait(barrier, 9)
            send(None, lout.at[way, rows], h1.at[way, rows], ring_recv.at[way, i], ahead[way])
    for way in range(2):
        send(None, lmeta.at[way], m1.at[way], meta_recv.at[way, 0], ahead[way])
    loads[3].wait()
    tell(0)
    def share(g, data, number, cell_id):
        length = number.shape[1]
        rel = number - 512 * z
        pick = (lax.broadcasted_iota(jnp.int32, (4 * CAP, length), 0) == rel).astype(F32).astype(BF16)
        packed = jnp.dot(pick, data, preferred_element_type=F32).astype(BF16)
        owner = (lax.broadcasted_iota(jnp.int32, (8, length), 0) == jnp.right_shift(rel, 7)).astype(F32)
        spot = (lax.broadcasted_iota(jnp.int32, (CAP, length), 0) == jnp.bitwise_and(rel, 127)).astype(F32).astype(BF16)
        cell_code = cell_id + 1
        high = jnp.right_shift(cell_code, 5).astype(F32)
        low = jnp.bitwise_and(cell_code, 31).astype(F32)
        chigh = lax.dot_general((owner * high).astype(BF16), spot, nt, preferred_element_type=F32)
        clow = lax.dot_general((owner * low).astype(BF16), spot, nt, preferred_element_type=F32)
        cells = (chigh * 32.0 + clow).astype(jnp.int32) - 1
        for k in range(4):
            scell[4 * g + k] = cells[k:k + 1, :]
            sbuf[g, k] = packed[CAP * k:CAP * k + CAP]
        for k in range(4):
            there = {"tile": z * 4 + k}
            send(k != kme, sbuf.at[g, k], rbuf.at[g, kme], rec_recv.at[g], there)
            send(k != kme, scell.at[4 * g + k], rcell.at[4 * g + kme], cell_recv.at[g], there)
        rbuf[g, kme] = sbuf[g, kme]
        rcell[4 * g + kme] = scell[4 * g + kme]

    def share_list(g, data, meta):
        share(g, data, jnp.right_shift(meta, 10), jnp.bitwise_and(meta, 1023))

    acc[...] = jnp.zeros_like(acc)
    dens[...] = jnp.zeros_like(dens)
    ones = jnp.ones((4 * CAP, 128), BF16)

    def chunk(g, ids, start):
        hit = (lax.broadcasted_iota(jnp.int32, (256, 4 * CAP), 0) + start == ids).astype(F32).astype(BF16)
        rows = pl.ds(start, 256)
        acc[rows, :] += jnp.dot(hit, rbuf[g].reshape(4 * CAP, 256), preferred_element_type=F32)
        dens[rows, :] += jnp.dot(hit, ones, preferred_element_type=F32)

    def group(g):
        arrived(rcell.at[pl.ds(4 * g, 3)], cell_recv.at[g])
        arrived(rbuf.at[g, pl.ds(0, 3)], rec_recv.at[g])
        return jnp.concatenate([rcell[4 * g + k] for k in range(4)], axis=1)

    def into_cells(g):
        ids = group(g)

        def step(r, _):
            chunk(g, ids, pl.multiple_of(r * 256, 256))
            return 0

        lax.fori_loop(0, 4, step, 0)

    share(0, rec[...], slot, cell)
    hear(0)
    tell(1)
    hear(1)
    tell(2)

    for way in range(2):
        arrived(m1.at[way], meta_recv.at[way, 0])
        send(None, m1.at[way], m2.at[way], meta_recv.at[way, 1], ahead[way])
    for i in (3, 2, 1, 0):
        rows = pl.ds(256 * i, 256)
        for way in range(2):
            arrived(h1.at[way, rows], ring_recv.at[way, i])
            send(None, h1.at[way, rows], h2.at[way, rows], ring_recv.at[way, 4 + i], ahead[way])
        if i == 3:
            hear(2)
            tell(3)
        if i == 2:
            hear(3)
            for n in FAR:
                yy = lax.rem(y + n, NY)
                send(active, wloc, wbuf.at[own_rows(dp)], w_recv, at(x, yy, z, c))
                send(active, wloc, wbuf.at[own_rows(dp)], w_recv, at(3 - x, yy, z, c))
            send(active, wloc, wbuf.at[own_rows(dp)], w_recv, at(3 - x, y, z, c))
    for way in range(2):
        share_list(1 + way, h1[way], m1[way])
    into_cells(0)

    for way in range(2):
        arrived(m2.at[way], meta_recv.at[way, 1])
        send(None, m2.at[way], m3.at[way], meta_recv.at[way, 2], ahead[way])
    for i in (3, 2, 1, 0):
        rows = pl.ds(256 * i, 256)
        for way in range(2):
            arrived(h2.at[way, rows], ring_recv.at[way, 4 + i])
            if i > 0:
                send(None, h2.at[way, rows], h3.at[way, pl.ds(256 * i - 256, 256)], ring_recv.at[way, 8 + i], ahead[way])
    for way in range(2):
        share_list(3 + way, h2[way], m2[way])
    into_cells(1)
    into_cells(2)

    for way in range(2):
        arrived(m3.at[way], meta_recv.at[way, 2])
        send(None, m3.at[way], m4.at[way], meta_recv.at[way, 3], ahead[way])
    for i in (3, 2, 1):
        rows = pl.ds(256 * i - 256, 256)
        for way in range(2):
            arrived(h3.at[way, rows], ring_recv.at[way, 8 + i])
            if i == 3:
                send(None, h3.at[way, rows], h4.at[way], ring_recv.at[way, 8], ahead[way])
    for way in range(2):
        share_list(5 + way, h3[way], m3[way][:, 256:1024])
    into_cells(3)
    into_cells(4)
    for way in range(2):
        arrived(m4.at[way], meta_recv.at[way, 3])
        arrived(h4.at[way], ring_recv.at[way, 8])
    share_list(7, h4[...].reshape(512, 256),
               jnp.concatenate([m4[0][:, 768:1024], m4[1][:, 768:1024]], axis=1))
    flush(len(started) - 24)
    into_cells(5)
    into_cells(6)

    @pl.when(active)
    def _():
        wbuf[own_rows(dp), :] = wloc[...]
        arrived(wbuf.at[pl.ds(0, 144 * (ndp // 2 - 1))], w_recv)

    @pl.when(jnp.logical_not(active))
    def _():
        arrived(wbuf.at[pl.ds(0, 144 * (ndp // 2))], w_recv)

    partner = at(x, y, z, 1 - c)
    for i in range(ndp // 2):
        rows = own_rows(2 * i + c)
        send(None, wbuf.at[rows], wbuf.at[rows], f_recv, partner)


    def block(n, size=256, count=1):
        return pl.ds(pl.multiple_of(n * size, size), size * count)

    def spread(e):
        value = xbuf[e].astype(F32)
        rmat[block(e), 0:256] = pltpu.roll(value, 1, 0).astype(BF16)
        rmat[block(e), 256:512] = value.astype(BF16)
        rmat[block(e), 512:768] = pltpu.roll(value, 255, 0).astype(BF16)

    rim = 9 * c
    at_end = (tile == 0) | (tile == NT - 1)
    inside = jnp.logical_not(at_end)
    own = 4 * c
    theirs = 4 - own
    out_row, in_row = 3 * c, 3 - 3 * c

    def finish(r):
        inv = 1.0 / (dens[block(r), :] + 1.0)
        value = acc[block(r), :] * jnp.concatenate([inv, inv], axis=1)
        xbuf[own + r + 1] = value.astype(BF16)

    def hand_over(r):
        e = own + r + 1
        send(None, xbuf.at[e], xbuf.at[e], x_recv.at[r], partner)

    g = 7
    ids = group(g)
    chunk(g, ids, pl.multiple_of(256 * out_row, 256))
    finish(out_row)
    send(inside, xbuf.at[own + out_row + 1], xbuf.at[9 - rim], h_recv, {"tile": tile - 1 + 2 * c})
    chunk(g, ids, pl.multiple_of(256 * in_row, 256))
    finish(in_row)
    hand_over(in_row)
    chunk(g, ids, 256)
    chunk(g, ids, 512)
    finish(1)
    finish(2)
    hand_over(1)
    hand_over(2)
    hand_over(out_row)
    for r in range(4):
        spread(own + r + 1)
    arrived(wbuf.at[pl.ds(0, 144 * (ndp // 2))], f_recv)
    loads[4].wait()

    def conv(r, n):
        pre = jnp.zeros((256 * n, 384), F32)
        for p in range(3):
            pre = pre + jnp.dot(rmat[block(own + r + p, count=n), :], wbuf[768 * p:768 * p + 768, :],
                                preferred_element_type=F32)
        c0 = 0.7978845608028654
        sq = pre * pre
        th = jnp.tanh(c0 * pre * (1.0 + 0.044715 * sq))
        slope = 0.5 * (1.0 + th) + 0.5 * pre * (1.0 - th * th) * (c0 * (1.0 + 3.0 * 0.044715 * sq))
        gp[block(own + r, count=n), :] = (cot[block(r, count=n), :].astype(F32) * slope).astype(BF16)

    def hand_gp(r, n, which):
        rows = block(own + r, count=n)
        send(None, gp.at[rows], gp.at[rows], g_recv.at[which], partner)

    def gp_arrived(n, which):
        arrived(gp.at[pl.ds(0, 256 * n)], g_recv.at[which])

    tn = (((0,), (0,)), ((), ()))

    taps = ((0, 0, 1, 2), (0, 1, 2, 0), (0, 2, 2, 1), (1, 0, 2, 2))

    def outer(row, n, fresh=False):
        right = gp[block(row, count=n), :]

        def put(rows, value):
            if fresh:
                grad[rows, :] = value
            else:
                grad[rows, :] += value

        for i, (p0, q0, p1, q1) in enumerate(taps):
            p = p0 + c * (p1 - p0)
            q = q0 + c * (q1 - q0)
            put(pl.ds(pl.multiple_of(256 * i + 128 * c, 128), 256), lax.dot_general(
                rmat[block(row + p, count=n), block(q)], right, tn, preferred_element_type=F32))
        put(pl.ds(pl.multiple_of(1024 - 1024 * c, 1024), 128), lax.dot_general(
            rmat[block(row + 1, count=n), block(2 + c, 128)], right, tn, preferred_element_type=F32))

    conv(1, 2)
    hand_gp(1, 2, 0)
    outer(own + 1, 2, fresh=True)
    arrived(xbuf.at[0], x_recv.at[out_row])
    spread(theirs + out_row + 1)
    conv(in_row, 1)
    hand_gp(in_row, 1, 1)
    for r in (1, 2):
        arrived(xbuf.at[0], x_recv.at[r])
        spread(theirs + r + 1)
    arrived(xbuf.at[0], x_recv.at[in_row])
    spread(theirs + in_row + 1)
    gp_arrived(2, 0)
    outer(theirs + 1, 2)
    gp_arrived(1, 1)
    outer(jnp.int32(3), 2)

    @pl.when(at_end)
    def _():
        xbuf[rim] = jnp.zeros((256, 256), BF16)

    @pl.when(inside)
    def _():
        arrived(xbuf.at[rim], h_recv)

    spread(rim)
    conv(out_row, 1)
    hand_gp(out_row, 1, 2)
    outer(own + out_row, 1)
    gp_arrived(1, 2)
    outer(theirs + in_row, 1)

    def stacked(value):
        return jnp.concatenate([value[:, 128 * b:128 * b + 128] for b in range(3)], axis=0)

    core0, core1 = c == 0, c == 1

    low_z = z < 7
    both = (c == xhi) & low_z
    before_sums = len(started)

    def convert(j):
        s2[j, 0:432] = stacked(grad[own_rows(j), :]).astype(BF16)
        s2[j, 432:448] = jnp.zeros((16, 128), BF16)

    halves = (pl.ds(0, 256), pl.ds(256, 176))

    @pl.when(core0)
    def _():
        for i in FAR:
            convert(lax.rem(y + i, NY))
        convert(y)
        ra2[y] = s2[y]

    for h in range(2):
        for i in FAR:
            j = lax.rem(y + i, NY)
            send(core0, s2.at[j, halves[h]], ra2.at[y, halves[h]], recvs.at[h], at(x, j, z, c))

    for h in range(2):
        fours = pl.ds(4 * h, 4)

        @pl.when(core1)
        def _(h=h, fours=fours):
            for j in range(4 * h, 4 * h + 4):
                convert(j)

            @pl.when(low_z)
            def _():
                for j in range(4 * h, 4 * h + 4):
                    rb2[z, j] = s2[j, block(z, 64)]

        for i in FAR:
            j = lax.rem(z + i, NZ)
            send(core1 & (j < 7), s2.at[fours, block(j, 64)], rb2.at[z, fours], recvs.at[2 + h], at(x, y, j, c))

    flush(before_sums)
    before_second = len(started)
    for h in range(2):
        first_piece, pieces = 4 * h, 4 - h

        @pl.when(core0)
        def _(h=h, first_piece=first_piece, pieces=pieces):
            arrived(ra2.at[pl.ds(0, 7), halves[h]], recvs.at[h])
            n = 256 - 80 * h
            total = ra2[0, 256 * h:256 * h + n].astype(F32)
            for i in range(1, 8):
                total = total + ra2[i, 256 * h:256 * h + n].astype(F32)
            if h == 1:
                total = jnp.concatenate([total, jnp.zeros((16, 128), F32)], axis=0)
            for j in range(pieces):
                p3[first_piece + j] = total[64 * j:64 * j + 64]

        for i in FAR:
            j = lax.rem(z + i, NZ)
            send(core0 & (j >= first_piece) & (j < first_piece + pieces), p3.at[j], r3.at[z], recvs.at[10], at(x, y, j, c))

        @pl.when(core1 & low_z)
        def _(h=h):
            arrived(rb2.at[pl.ds(0, 7), pl.ds(4 * h, 4)], recvs.at[2 + h])
            for j in range(4 * h, 4 * h + 4):
                total = rb2[0, j].astype(F32)
                for i in range(1, 8):
                    total = total + rb2[i, j].astype(F32)
                p3[j] = total

        for i in FAR:
            j = lax.rem(y + i, NY)
            send(core1 & low_z & (lax.div(j, 4) == h), p3.at[j], r3.at[y], recvs.at[11], at(x, j, z, c))

    flush(before_second)

    @pl.when(core0 & low_z)
    def _():
        r3[z] = p3[z]
        arrived(r3.at[pl.ds(0, 7)], recvs.at[10])

    @pl.when(core1 & low_z)
    def _():
        r3[y] = p3[y]
        arrived(r3.at[pl.ds(0, 7)], recvs.at[11])

    @pl.when(low_z)
    def _():
        total = r3[0]
        for i in range(1, 8):
            total = total + r3[i]
        q4[...] = total

    for i in range(2):
        xx = 2 * c + i
        send(low_z & (xx != x), q4, r4.at[x], recvs.at[12], at(xx, y, z, c))

    flush(len(started) - 2)

    @pl.when(both)
    def _():
        r4[x] = q4[...]

    @pl.when(both)
    def _():
        arrived(r4.at[pl.ds(0, 3)], recvs.at[12])
        f5[z] = ((r4[0] + r4[1]) + (r4[2] + r4[3])).astype(BF16)

    for i in FAR + (0,):
        zz = lax.rem(z + i, NZ)
        for cc in ((1 - c,) if i == 0 else (c, 1 - c)):
            send(both, f5.at[z], f5.at[z], recvs.at[13], at(x, y, zz, cc))

    flush(len(started) - 15)

    @pl.when(both)
    def _():
        arrived(f5.at[pl.ds(0, 6)], recvs.at[13])

    @pl.when(jnp.logical_not(both))
    def _():
        arrived(f5, recvs.at[13])

    done = f5[...].astype(F32).reshape(448, 128)
    for b in range(3):
        out_ref[:, 128 * b:128 * b + 128] = done[144 * b:144 * b + 144]

    flush(len(started))


def local(records, obs_tile, obs_cell, conv_weight, cotangent):
    dma = pltpu.SemaphoreType.DMA
    any_space = pl.BlockSpec(memory_space=pl.ANY)

    def half(*shape):
        return pltpu.VMEM(shape, BF16)

    def full(*shape):
        return pltpu.VMEM(shape, F32)

    def ints(*shape):
        return pltpu.VMEM(shape, jnp.int32)

    return pl.pallas_call(
        fused,
        out_shape=jax.ShapeDtypeStruct((144, 384), F32),
        in_specs=[any_space] * 5,
        out_specs=pl.BlockSpec(memory_space=pltpu.VMEM),
        scratch_shapes=[
            half(1024, 256), ints(1, 1024), ints(1, 1024), half(144, 384), half(1024, 384),
            half(2, 1024, 256), ints(2, 1, 1024), half(2, 1024, 256), half(2, 1024, 256), half(2, 768, 256),
            half(2, 256, 256), ints(2, 1, 1024), ints(2, 1, 1024), ints(2, 1, 1024), ints(2, 1, 1024),
            half(NZ, 4, CAP, 256), ints(NT, 1, CAP), half(NZ, 4, CAP, 256), ints(NT, 1, CAP),
            half(2304, 384), half(10, 256, 256), half(2560, 768), full(1024, 256), full(1024, 128),
            half(2048, 384), full(1152, 384),
            half(8, 448, 128), half(8, 448, 128), half(8, 8, 64, 128), full(8, 64, 128),
            full(8, 64, 128), full(64, 128), full(4, 64, 128), half(7, 64, 128),
            dma((5,)), pltpu.SemaphoreType.REGULAR((4,)), dma((240,)), dma((2, 12)), dma((2, 4)), dma((NZ,)), dma((NZ,)), dma, dma, dma, dma((4,)), dma((3,)), dma((16,)),
        ],
        compiler_params=pltpu.CompilerParams(
            collective_id=0, has_side_effects=True, vmem_limit_bytes=58 * 1024 * 1024),
    )(records[0], obs_tile.reshape(1, 1024), obs_cell, conv_weight, cotangent.reshape(1024, 384))


def solution(mesh):
    placed = (
        P("dp", "tile", None),
        P("dp", "tile", None),
        P("dp", "tile"),
        P("dp", None),
        P("dp", "tile", None, None),
    )
    return jax.shard_map(
        local, mesh=mesh, in_specs=placed, out_specs=P("dp", None), check_vma=False
    )
```

```python
import jax
import jax.numpy as jnp
from jax import lax
from jax.experimental import pallas as pl
from jax.experimental.pallas import tpu as pltpu
from jax.sharding import PartitionSpec as P

MESH = pl.DeviceIdType.MESH
F32 = jnp.float32
BF16 = jnp.bfloat16
NZ = 8
NY = 8
NT = 32
CAP = 128
FAR = (4, 3, 5, 2, 6, 1, 7)


def remote(src, dst, send, recv, where):
    return pltpu.make_async_remote_copy(
        src_ref=src, dst_ref=dst, send_sem=send, recv_sem=recv,
        device_id=where, device_id_type=MESH,
    )


def fused(rec_hbm, tile_hbm, cell_hbm, w_hbm, cot_hbm, out_ref,
          rec, til, cel, wloc, cot,
          lout, lmeta, h1, h2, h3, h4, m1, m2, m3, m4, sbuf, scell, rbuf, rcell, wbuf, xbuf, rmat, acc, dens, gp, grad,
          s2, ra2, rb2, p3, r3, q4, r4, f5,
          local_sem, news, sends, ring_recv, meta_recv, rec_recv, cell_recv, w_recv, f_recv, h_recv, x_recv, g_recv, recvs):
    tile = lax.axis_index("tile")
    dp = lax.axis_index("dp")
    z = lax.div(tile, 4)
    kme = lax.rem(tile, 4)
    xlo = lax.div(kme, 2)
    c = lax.rem(tile, 2)
    y = lax.rem(dp, NY)
    xhi = lax.div(dp, NY)
    x = xhi * 2 + xlo
    ndp = 2 * NY
    me = {"tile": tile}

    def at(xx, yy, zz, cc):
        return {"dp": lax.div(xx, 2) * NY + yy, "tile": zz * 4 + lax.rem(xx, 2) * 2 + cc}

    def arrived(ref, sem):
        remote(ref, ref, sem, sem, me).wait_recv()

    started = []

    def under(cond, act):
        if cond is None:
            act()
        else:
            pl.when(cond)(act)

    def send(cond, src, dst, recv, where):
        n = len(started)

        def copy():
            return remote(src, dst, sends.at[n], recv, where)

        started.append((cond, copy))
        under(cond, lambda: copy().start())

    loads = [pltpu.make_async_copy(a, b, local_sem.at[i]) for i, (a, b) in enumerate(
        ((tile_hbm, til), (cell_hbm, cel), (rec_hbm, rec), (w_hbm, wloc), (cot_hbm, cot)))]
    for load in loads:
        load.start()

    flushed = [0]

    def flush(upto):
        for cond, copy in started[flushed[0]:upto]:
            under(cond, lambda copy=copy: copy().wait_send())
        flushed[0] = upto

    barrier = pltpu.get_barrier_semaphore()

    def greet(where):
        pl.semaphore_signal(barrier, inc=1, device_id=where, device_id_type=MESH)

    ahead = ({"tile": lax.rem(tile + 4, NT)}, {"tile": lax.rem(tile + NT - 4, NT)})
    beside = (at(x, lax.rem(y + 1, NY), z, c), at(x, lax.rem(y + NY - 1, NY), z, c))
    for where in ahead + beside:
        greet(where)
    for k in range(1, 4):
        greet({"tile": z * 4 + lax.rem(kme + k, 4)})
    greet(at(lax.rem(x + 2, 4), y, z, c))
    greet(at(3 - x, y, z, c))

    def tell(n):
        for where in ahead + beside:
            pl.semaphore_signal(news.at[n], inc=1, device_id=where, device_id_type=MESH)

    def hear(n):
        pl.semaphore_wait(news.at[n], 4)

    loads[0].wait()
    loads[1].wait()

    dest = til[...]
    marks = (lax.broadcasted_iota(jnp.int32, (NT, 1024), 0) == dest).astype(F32)
    upper = (lax.broadcasted_iota(jnp.int32, (256, 256), 0)
             < lax.broadcasted_iota(jnp.int32, (256, 256), 1)).astype(F32).astype(BF16)
    carry = jnp.zeros((NT, 1), F32)
    parts = []
    for i in range(4):
        m = marks[:, 256 * i:256 * i + 256]
        parts.append(jnp.dot(m.astype(BF16), upper, preferred_element_type=F32) + carry)
        carry = carry + jnp.sum(m, axis=1, keepdims=True)
    before = jnp.concatenate(parts, axis=1)
    pos = jnp.sum(before * marks, axis=0, keepdims=True).astype(jnp.int32)
    slot = dest * CAP + pos
    nt = (((1,), (1,)), ((), ()))

    def key(axis, shape, way):
        t = lax.broadcasted_iota(jnp.int32, shape, axis)
        away = jnp.bitwise_and(jnp.right_shift(t, 2) - z, 7)
        if way == 1:
            away = jnp.bitwise_and(8 - away, 7)
        limit = jnp.where(jnp.bitwise_and(t, 1) == way, 4, 3)
        return jnp.where((away >= 1) & (away <= limit), away * NT + t, -1)

    total_b = jnp.broadcast_to(carry, (NT, 128)).astype(BF16)
    spots = []
    for way in range(2):
        down, across = key(0, (NT, NT), way), key(1, (NT, NT), way)
        later = (across > down).astype(F32).astype(BF16)
        offset = jnp.dot(later, total_b, preferred_element_type=F32)[:, 0:1]
        base = jnp.where(key(0, (NT, 1), way) >= 0, 1024.0 - offset - carry, -4096.0)
        spots.append(jnp.sum((base + before) * marks, axis=0, keepdims=True).astype(jnp.int32))
    code = slot + 1
    cell = cel[...]
    traits = jnp.concatenate([
        jnp.right_shift(code, 6).astype(F32), jnp.bitwise_and(code, 63).astype(F32),
        jnp.right_shift(cell, 5).astype(F32), jnp.bitwise_and(cell, 31).astype(F32),
        jnp.zeros((4, 1024), F32)], axis=0).astype(BF16)
    loads[2].wait()

    def own_rows(d):
        return pl.ds(pl.multiple_of(144 * d, 16), 144)

    active = lax.rem(dp + c, 2) == 0
    for i in (3, 2, 1, 0):
        for way in range(2):
            rows = pl.ds(256 * i, 256)
            perm = (lax.broadcasted_iota(jnp.int32, (256, 1024), 0) + 256 * i == spots[way]).astype(F32).astype(BF16)
            lout[way, rows] = jnp.dot(perm, rec[...], preferred_element_type=F32).astype(BF16)
            got = lax.dot_general(traits, perm, nt, preferred_element_type=F32)
            number = (got[0:1] * 64.0 + got[1:2]).astype(jnp.int32) - 1
            lmeta[way, :, rows] = number * 1024 + (got[2:3] * 32.0 + got[3:4]).astype(jnp.int32)
            if i == 3 and way == 0:
                pl.semaphore_wait(barrier, 9)
            send(None, lout.at[way, rows], h1.at[way, rows], ring_recv.at[way, i], ahead[way])
    for way in range(2):
        send(None, lmeta.at[way], m1.at[way], meta_recv.at[way, 0], ahead[way])
    loads[3].wait()
    tell(0)
    def share(g, data, number, cell_id):
        length = number.shape[1]
        rel = number - 512 * z
        pick = (lax.broadcasted_iota(jnp.int32, (4 * CAP, length), 0) == rel).astype(F32).astype(BF16)
        packed = jnp.dot(pick, data, preferred_element_type=F32).astype(BF16)
        owner = (lax.broadcasted_iota(jnp.int32, (8, length), 0) == jnp.right_shift(rel, 7)).astype(F32)
        spot = (lax.broadcasted_iota(jnp.int32, (CAP, length), 0) == jnp.bitwise_and(rel, 127)).astype(F32).astype(BF16)
        cell_code = cell_id + 1
        high = jnp.right_shift(cell_code, 5).astype(F32)
        low = jnp.bitwise_and(cell_code, 31).astype(F32)
        chigh = lax.dot_general((owner * high).astype(BF16), spot, nt, preferred_element_type=F32)
        clow = lax.dot_general((owner * low).astype(BF16), spot, nt, preferred_element_type=F32)
        cells = (chigh * 32.0 + clow).astype(jnp.int32) - 1
        for k in range(4):
            scell[4 * g + k] = cells[k:k + 1, :]
            sbuf[g, k] = packed[CAP * k:CAP * k + CAP]
        turn = 1 - 2 * lax.rem(kme, 2)
        across = lax.rem(kme + 2, 4)
        for k in (across, across + turn, kme + turn):
            there = {"tile": z * 4 + k}
            send(None, sbuf.at[g, k], rbuf.at[g, kme], rec_recv.at[g], there)
            send(None, scell.at[4 * g + k], rcell.at[4 * g + kme], cell_recv.at[g], there)
        rbuf[g, kme] = sbuf[g, kme]
        rcell[4 * g + kme] = scell[4 * g + kme]

    def share_list(g, data, meta):
        share(g, data, jnp.right_shift(meta, 10), jnp.bitwise_and(meta, 1023))

    acc[...] = jnp.zeros_like(acc)
    dens[...] = jnp.zeros_like(dens)
    ones = jnp.ones((4 * CAP, 128), BF16)

    def chunk(g, ids, start):
        hit = (lax.broadcasted_iota(jnp.int32, (256, 4 * CAP), 0) + start == ids).astype(F32).astype(BF16)
        rows = pl.ds(start, 256)
        acc[rows, :] += jnp.dot(hit, rbuf[g].reshape(4 * CAP, 256), preferred_element_type=F32)
        dens[rows, :] += jnp.dot(hit, ones, preferred_element_type=F32)

    def group(g):
        arrived(rcell.at[pl.ds(4 * g, 3)], cell_recv.at[g])
        arrived(rbuf.at[g, pl.ds(0, 3)], rec_recv.at[g])
        return jnp.concatenate([rcell[4 * g + k] for k in range(4)], axis=1)

    def into_cells(g):
        ids = group(g)

        def step(r, _):
            chunk(g, ids, pl.multiple_of(r * 256, 256))
            return 0

        lax.fori_loop(0, 4, step, 0)

    share(0, rec[...], slot, cell)
    hear(0)
    tell(1)
    hear(1)
    tell(2)

    for i in (3, 2, 1, 0):
        rows = pl.ds(256 * i, 256)
        for way in range(2):
            arrived(h1.at[way, rows], ring_recv.at[way, i])
            send(None, h1.at[way, rows], h2.at[way, rows], ring_recv.at[way, 4 + i], ahead[way])
        if i == 3:
            hear(2)
            tell(3)
        if i == 2:
            hear(3)
            for n in FAR:
                yy = lax.rem(y + n, NY)
                send(active, wloc, wbuf.at[own_rows(dp)], w_recv, at(x, yy, z, c))
                send(active, wloc, wbuf.at[own_rows(dp)], w_recv, at(3 - x, yy, z, c))
            send(active, wloc, wbuf.at[own_rows(dp)], w_recv, at(3 - x, y, z, c))
    for way in range(2):
        arrived(m1.at[way], meta_recv.at[way, 0])
        send(None, m1.at[way], m2.at[way], meta_recv.at[way, 1], ahead[way])
    for way in range(2):
        share_list(1 + way, h1[way], m1[way])
    into_cells(0)

    for i in (3, 2, 1, 0):
        rows = pl.ds(256 * i, 256)
        for way in range(2):
            arrived(h2.at[way, rows], ring_recv.at[way, 4 + i])
            if i > 0:
                send(None, h2.at[way, rows], h3.at[way, pl.ds(256 * i - 256, 256)], ring_recv.at[way, 8 + i], ahead[way])
    for way in range(2):
        arrived(m2.at[way], meta_recv.at[way, 1])
        send(None, m2.at[way], m3.at[way], meta_recv.at[way, 2], ahead[way])
    for way in range(2):
        share_list(3 + way, h2[way], m2[way])
    into_cells(1)
    into_cells(2)

    for i in (3, 2, 1):
        rows = pl.ds(256 * i - 256, 256)
        for way in range(2):
            arrived(h3.at[way, rows], ring_recv.at[way, 8 + i])
            if i == 3:
                send(None, h3.at[way, rows], h4.at[way], ring_recv.at[way, 8], ahead[way])
    for way in range(2):
        arrived(m3.at[way], meta_recv.at[way, 2])
        send(None, m3.at[way], m4.at[way], meta_recv.at[way, 3], ahead[way])
    for way in range(2):
        share_list(5 + way, h3[way], m3[way][:, 256:1024])
    into_cells(3)
    into_cells(4)
    for way in range(2):
        arrived(m4.at[way], meta_recv.at[way, 3])
        arrived(h4.at[way], ring_recv.at[way, 8])
    share_list(7, h4[...].reshape(512, 256),
               jnp.concatenate([m4[0][:, 768:1024], m4[1][:, 768:1024]], axis=1))
    flush(len(started) - 18)
    into_cells(5)
    into_cells(6)

    @pl.when(active)
    def _():
        wbuf[own_rows(dp), :] = wloc[...]
        arrived(wbuf.at[pl.ds(0, 144 * (ndp // 2 - 1))], w_recv)

    @pl.when(jnp.logical_not(active))
    def _():
        arrived(wbuf.at[pl.ds(0, 144 * (ndp // 2))], w_recv)

    partner = at(x, y, z, 1 - c)
    for i in range(ndp // 2):
        rows = own_rows(2 * i + c)
        send(None, wbuf.at[rows], wbuf.at[rows], f_recv, partner)


    def block(n, size=256, count=1):
        return pl.ds(pl.multiple_of(n * size, size), size * count)

    def spread(e):
        value = xbuf[e].astype(F32)
        rmat[block(e), 0:256] = pltpu.roll(value, 1, 0).astype(BF16)
        rmat[block(e), 256:512] = value.astype(BF16)
        rmat[block(e), 512:768] = pltpu.roll(value, 255, 0).astype(BF16)

    rim = 9 * c
    at_end = (tile == 0) | (tile == NT - 1)
    inside = jnp.logical_not(at_end)
    own = 4 * c
    theirs = 4 - own
    out_row, in_row = 3 * c, 3 - 3 * c

    def finish(r):
        inv = 1.0 / (dens[block(r), :] + 1.0)
        value = acc[block(r), :] * jnp.concatenate([inv, inv], axis=1)
        xbuf[own + r + 1] = value.astype(BF16)

    def hand_over(r):
        e = own + r + 1
        send(None, xbuf.at[e], xbuf.at[e], x_recv.at[r], partner)

    g = 7
    ids = group(g)
    chunk(g, ids, pl.multiple_of(256 * out_row, 256))
    finish(out_row)
    send(inside, xbuf.at[own + out_row + 1], xbuf.at[9 - rim], h_recv, {"tile": tile - 1 + 2 * c})
    chunk(g, ids, pl.multiple_of(256 * in_row, 256))
    finish(in_row)
    hand_over(in_row)
    chunk(g, ids, 256)
    chunk(g, ids, 512)
    finish(1)
    finish(2)
    hand_over(1)
    hand_over(2)
    hand_over(out_row)
    for r in range(4):
        spread(own + r + 1)
    arrived(wbuf.at[pl.ds(0, 144 * (ndp // 2))], f_recv)
    loads[4].wait()

    def conv(r, n):
        pre = jnp.zeros((256 * n, 384), F32)
        for p in range(3):
            pre = pre + jnp.dot(rmat[block(own + r + p, count=n), :], wbuf[768 * p:768 * p + 768, :],
                                preferred_element_type=F32)
        c0 = 0.7978845608028654
        sq = pre * pre
        th = jnp.tanh(c0 * pre * (1.0 + 0.044715 * sq))
        slope = 0.5 * (1.0 + th) + 0.5 * pre * (1.0 - th * th) * (c0 * (1.0 + 3.0 * 0.044715 * sq))
        gp[block(own + r, count=n), :] = (cot[block(r, count=n), :].astype(F32) * slope).astype(BF16)

    def hand_gp(r, n, which):
        rows = block(own + r, count=n)
        send(None, gp.at[rows], gp.at[rows], g_recv.at[which], partner)

    def gp_arrived(n, which):
        arrived(gp.at[pl.ds(0, 256 * n)], g_recv.at[which])

    tn = (((0,), (0,)), ((), ()))

    taps = ((0, 0, 1, 2), (0, 1, 2, 0), (0, 2, 2, 1), (1, 0, 2, 2))

    def outer(row, n, fresh=False):
        right = gp[block(row, count=n), :]

        def put(rows, value):
            if fresh:
                grad[rows, :] = value
            else:
                grad[rows, :] += value

        for i, (p0, q0, p1, q1) in enumerate(taps):
            p = p0 + c * (p1 - p0)
            q = q0 + c * (q1 - q0)
            put(pl.ds(pl.multiple_of(256 * i + 128 * c, 128), 256), lax.dot_general(
                rmat[block(row + p, count=n), block(q)], right, tn, preferred_element_type=F32))
        put(pl.ds(pl.multiple_of(1024 - 1024 * c, 1024), 128), lax.dot_general(
            rmat[block(row + 1, count=n), block(2 + c, 128)], right, tn, preferred_element_type=F32))

    conv(1, 2)
    hand_gp(1, 2, 0)
    outer(own + 1, 2, fresh=True)
    arrived(xbuf.at[0], x_recv.at[out_row])
    spread(theirs + out_row + 1)
    conv(in_row, 1)
    hand_gp(in_row, 1, 1)
    for r in (1, 2):
        arrived(xbuf.at[0], x_recv.at[r])
        spread(theirs + r + 1)
    arrived(xbuf.at[0], x_recv.at[in_row])
    spread(theirs + in_row + 1)
    gp_arrived(2, 0)
    outer(theirs + 1, 2)
    gp_arrived(1, 1)
    outer(jnp.int32(3), 2)

    @pl.when(at_end)
    def _():
        xbuf[rim] = jnp.zeros((256, 256), BF16)

    @pl.when(inside)
    def _():
        arrived(xbuf.at[rim], h_recv)

    spread(rim)
    conv(out_row, 1)
    hand_gp(out_row, 1, 2)
    outer(own + out_row, 1)
    gp_arrived(1, 2)
    outer(theirs + in_row, 1)

    def stacked(value):
        return jnp.concatenate([value[:, 128 * b:128 * b + 128] for b in range(3)], axis=0)

    core0, core1 = c == 0, c == 1

    low_z = z < 7
    both = (c == xhi) & low_z
    before_sums = len(started)

    def convert(j):
        s2[j, 0:432] = stacked(grad[own_rows(j), :]).astype(BF16)
        s2[j, 432:448] = jnp.zeros((16, 128), BF16)

    halves = (pl.ds(0, 256), pl.ds(256, 176))

    @pl.when(core0)
    def _():
        for i in FAR:
            convert(lax.rem(y + i, NY))
        convert(y)
        ra2[y] = s2[y]

    for h in range(2):
        for i in FAR:
            j = lax.rem(y + i, NY)
            send(core0, s2.at[j, halves[h]], ra2.at[y, halves[h]], recvs.at[h], at(x, j, z, c))

    for h in range(2):
        fours = pl.ds(4 * h, 4)

        @pl.when(core1)
        def _(h=h, fours=fours):
            for j in range(4 * h, 4 * h + 4):
                convert(j)

            @pl.when(low_z)
            def _():
                for j in range(4 * h, 4 * h + 4):
                    rb2[z, j] = s2[j, block(z, 64)]

        for i in FAR:
            j = lax.rem(z + i, NZ)
            send(core1 & (j < 7), s2.at[fours, block(j, 64)], rb2.at[z, fours], recvs.at[2 + h], at(x, y, j, c))

    flush(before_sums)
    before_second = len(started)
    for h in range(2):
        first_piece, pieces = 4 * h, 4 - h

        @pl.when(core0)
        def _(h=h, first_piece=first_piece, pieces=pieces):
            arrived(ra2.at[pl.ds(0, 7), halves[h]], recvs.at[h])
            n = 256 - 80 * h
            total = ra2[0, 256 * h:256 * h + n].astype(F32)
            for i in range(1, 8):
                total = total + ra2[i, 256 * h:256 * h + n].astype(F32)
            if h == 1:
                total = jnp.concatenate([total, jnp.zeros((16, 128), F32)], axis=0)
            for j in range(pieces):
                p3[first_piece + j] = total[64 * j:64 * j + 64]

        for i in FAR:
            j = lax.rem(z + i, NZ)
            send(core0 & (j >= first_piece) & (j < first_piece + pieces), p3.at[j], r3.at[z], recvs.at[10], at(x, y, j, c))

        @pl.when(core1 & low_z)
        def _(h=h):
            arrived(rb2.at[pl.ds(0, 7), pl.ds(4 * h, 4)], recvs.at[2 + h])
            for j in range(4 * h, 4 * h + 4):
                total = rb2[0, j].astype(F32)
                for i in range(1, 8):
                    total = total + rb2[i, j].astype(F32)
                p3[j] = total

        for i in FAR:
            j = lax.rem(y + i, NY)
            send(core1 & low_z & (lax.div(j, 4) == h), p3.at[j], r3.at[y], recvs.at[11], at(x, j, z, c))

    flush(before_second)

    @pl.when(core0 & low_z)
    def _():
        r3[z] = p3[z]
        arrived(r3.at[pl.ds(0, 7)], recvs.at[10])

    @pl.when(core1 & low_z)
    def _():
        r3[y] = p3[y]
        arrived(r3.at[pl.ds(0, 7)], recvs.at[11])

    @pl.when(low_z)
    def _():
        total = r3[0]
        for i in range(1, 8):
            total = total + r3[i]
        q4[...] = total

    for i in range(2):
        xx = 2 * c + i
        send(low_z & (xx != x), q4, r4.at[x], recvs.at[12], at(xx, y, z, c))

    flush(len(started) - 2)

    @pl.when(both)
    def _():
        r4[x] = q4[...]

    @pl.when(both)
    def _():
        arrived(r4.at[pl.ds(0, 3)], recvs.at[12])
        f5[z] = ((r4[0] + r4[1]) + (r4[2] + r4[3])).astype(BF16)

    for i in FAR + (0,):
        zz = lax.rem(z + i, NZ)
        for cc in ((1 - c,) if i == 0 else (c, 1 - c)):
            send(both, f5.at[z], f5.at[z], recvs.at[13], at(x, y, zz, cc))

    flush(len(started) - 15)

    @pl.when(both)
    def _():
        arrived(f5.at[pl.ds(0, 6)], recvs.at[13])

    @pl.when(jnp.logical_not(both))
    def _():
        arrived(f5, recvs.at[13])

    done = f5[...].astype(F32).reshape(448, 128)
    for b in range(3):
        out_ref[:, 128 * b:128 * b + 128] = done[144 * b:144 * b + 144]

    flush(len(started))


def local(records, obs_tile, obs_cell, conv_weight, cotangent):
    dma = pltpu.SemaphoreType.DMA
    any_space = pl.BlockSpec(memory_space=pl.ANY)

    def half(*shape):
        return pltpu.VMEM(shape, BF16)

    def full(*shape):
        return pltpu.VMEM(shape, F32)

    def ints(*shape):
        return pltpu.VMEM(shape, jnp.int32)

    return pl.pallas_call(
        fused,
        out_shape=jax.ShapeDtypeStruct((144, 384), F32),
        in_specs=[any_space] * 5,
        out_specs=pl.BlockSpec(memory_space=pltpu.VMEM),
        scratch_shapes=[
            half(1024, 256), ints(1, 1024), ints(1, 1024), half(144, 384), half(1024, 384),
            half(2, 1024, 256), ints(2, 1, 1024), half(2, 1024, 256), half(2, 1024, 256), half(2, 768, 256),
            half(2, 256, 256), ints(2, 1, 1024), ints(2, 1, 1024), ints(2, 1, 1024), ints(2, 1, 1024),
            half(NZ, 4, CAP, 256), ints(NT, 1, CAP), half(NZ, 4, CAP, 256), ints(NT, 1, CAP),
            half(2304, 384), half(10, 256, 256), half(2560, 768), full(1024, 256), full(1024, 128),
            half(2048, 384), full(1152, 384),
            half(8, 448, 128), half(8, 448, 128), half(8, 8, 64, 128), full(8, 64, 128),
            full(8, 64, 128), full(64, 128), full(4, 64, 128), half(7, 64, 128),
            dma((5,)), pltpu.SemaphoreType.REGULAR((4,)), dma((240,)), dma((2, 12)), dma((2, 4)), dma((NZ,)), dma((NZ,)), dma, dma, dma, dma((4,)), dma((3,)), dma((16,)),
        ],
        compiler_params=pltpu.CompilerParams(
            collective_id=0, has_side_effects=True, vmem_limit_bytes=58 * 1024 * 1024),
    )(records[0], obs_tile.reshape(1, 1024), obs_cell, conv_weight, cotangent.reshape(1024, 384))


def solution(mesh):
    placed = (
        P("dp", "tile", None),
        P("dp", "tile", None),
        P("dp", "tile"),
        P("dp", None),
        P("dp", "tile", None, None),
    )
    return jax.shard_map(
        local, mesh=mesh, in_specs=placed, out_specs=P("dp", None), check_vma=False
    )
```
